256 devices in a mesh: blk: 128 (over z, x, y), rep: 2 (over core).
Axes of the slice: x: 4, y: 4, z: 8, core: 2. Of those that a mesh axis runs over, the one named last changes fastest.
Arguments:
- right_side: float32 [8, 262144], P(None, 'blk'), may hold values from -6 to 6
- coords: float32 [3, 262144], P(None, 'blk'), as said below
- counts: int32 [512], P('blk'), may hold values from 128 to 512
- pair_list: int32 [3, 2560], P(None, ('blk', 'rep')), may hold values from 0 to 511, as said below
Outputs:
- solution: float32 [8, 262144], P(None, 'blk')
- residual: float32 [8, 262144], P(None, 'blk')
The draws below stay inside these ranges and needn't reach their ends.
Inputs may be any that keep to these rules, and one draw needn't show every extreme that they name: `pair_list`: row 0 holds a row block, row 1 a partner block from the row block to 4 blocks after it, row 2 is 1 for a live pair and 0 for an empty slot. The live pairs are exactly the block pairs, each once with the lower block as row block, whose locations can lie closer than 4; all other block pairs have every distance 4 or more. The blocks of group g, 4 g to 4 g + 3, own slots 2 * 10 g onwards, 20 of them, live pairs first; an empty slot names the group's first block twice. Some row block has a partner exactly 4 blocks after it. `coords`: each block's locations lie in a slab along the first coordinate, blocks in increasing order without gaps; second and third coordinates between 0 and 1.
All inputs are finite; a program needn't handle non-finite values.
Results may differ from the reference program's by a relative error of at most 0.0003.
Values sent between devices are 32-bit elements; how exact they have to be, the bound alone decides.
A program may use at most 64 MiB of HBM per device.

```python
import math
import jax
import jax.numpy as jnp
from jax import lax

TILE = 512
PROBES = 8
ITERS = 2
BLK_DEV = 4
SPAN = 4
NBLK = 512
NLOC = 262144


def block_widths(key):
    widths = jax.random.randint(key, (NBLK,), 1, 3)
    blocks = jnp.arange(NBLK)
    forced = (blocks >= 1) & (blocks < SPAN)
    return jnp.where(forced, 1, widths).astype(jnp.int32)


def draw_pair_list(key, part):
    widths = block_widths(key)
    starts = jnp.cumsum(widths) - widths
    blocks = jnp.arange(NBLK, dtype=jnp.int32)
    offsets = jnp.arange(SPAN + 1, dtype=jnp.int32)
    partner = blocks[:, None] + offsets[None, :]
    bounded = jnp.minimum(partner, NBLK - 1)
    spacing = starts[bounded] - starts[:, None] - widths[:, None]
    living = (partner < NBLK) & ((offsets[None, :] == 0) | (spacing < SPAN))
    groups = NBLK // BLK_DEV
    living = living.reshape(groups, BLK_DEV * (SPAN + 1)).astype(jnp.int32)
    row_ids = jnp.broadcast_to(blocks[:, None], partner.shape).reshape(groups, -1)
    col_ids = bounded.reshape(groups, -1)
    order = jnp.argsort(1 - living, axis=1, stable=True)
    living = jnp.take_along_axis(living, order, axis=1)
    row_ids = jnp.take_along_axis(row_ids, order, axis=1)
    col_ids = jnp.take_along_axis(col_ids, order, axis=1)
    first = (jnp.arange(groups, dtype=jnp.int32) * BLK_DEV)[:, None]
    row_ids = jnp.where(living == 1, row_ids, first)
    col_ids = jnp.where(living == 1, col_ids, first)
    return jnp.stack([row_ids.reshape(-1), col_ids.reshape(-1), living.reshape(-1)]).astype(jnp.int32)


def draw_coords(key, part):
    widths = block_widths(key)
    starts = jnp.cumsum(widths) - widths
    key = jax.random.fold_in(key, 5)
    first_key, second_key = jax.random.split(key)
    along = jax.random.uniform(first_key, (NBLK, TILE), jnp.float32)
    across = jax.random.uniform(second_key, (2, NBLK, TILE), jnp.float32)
    position = starts[:, None].astype(jnp.float32) + along * widths[:, None].astype(jnp.float32)
    stacked = jnp.concatenate([position[None], across], axis=0)
    return stacked.reshape(3, NBLK * TILE).astype(jnp.float32)


def with_ends(entries, rng, low, top_value):
    shape = entries.shape
    place = [jax.random.randint(jax.random.fold_in(rng, axis), (), 0, shape[axis]) for axis in range(len(shape))]
    entries = entries.at[tuple(place)].set(low)
    longest = shape.index(max(shape))
    place[longest] = (place[longest] + 1) % shape[longest]
    return entries.at[tuple(place)].set(top_value)


def block_levels(stream_key, shape, shards, smallest, high):
    factor_of = 1.0
    for dim, blocks in shards:
        draws = jax.random.uniform(jax.random.fold_in(jax.random.fold_in(stream_key, 6), dim), (blocks,), jnp.float32, smallest / len(shards), high / len(shards))
        factor_of = factor_of * jnp.repeat(jnp.exp(draws), shape[dim] // blocks).reshape((-1,) + (1,) * (len(shape) - 1 - dim))
    return factor_of


def centred(stream_key, shape, deviation, limit, cuts=(), kind=jnp.bfloat16):
    gain = block_levels(stream_key, shape, cuts, -0.22, 0.18) if cuts else 1.0
    values = jax.random.normal(stream_key, shape, jnp.float32) * deviation * gain
    return jnp.minimum(jnp.maximum(values, -limit), limit).astype(kind)


def setup_inputs(seed: int = 0) -> dict:
    streams_of = jax.random.split(jax.random.key(seed), 5)
    return {
        "right_side": centred(streams_of[0], (PROBES, NLOC), 1.0, 6.0, ((1, 128),), jnp.float32),
        "coords": draw_coords(jax.random.fold_in(streams_of[4], 71), 0),
        "counts": with_ends(jax.random.randint(streams_of[2], (NBLK,), TILE // 4, TILE + 1), jax.random.fold_in(streams_of[2], 1), TILE // 4, TILE).astype(jnp.int32),
        "pair_list": draw_pair_list(jax.random.fold_in(streams_of[4], 71), 0),
    }


sill_factor = 0.1
range_factor = 0.5
nugget = 0.5
highest = lax.Precision.HIGHEST

def cov_tile(left, right, left_alive, right_alive, taper_radius):
    diff = left[:, :, None] - right[:, None, :]
    dist = jnp.sqrt(lax.optimization_barrier(jnp.sum(diff * diff, axis=0)))
    scaled = dist * (math.sqrt(3.0) / (range_factor * taper_radius))
    matern = (1.0 + scaled) * jnp.exp(-scaled)
    ratio = dist / taper_radius
    taper = jnp.maximum(1.0 - ratio, 0.0)
    taper = taper * taper * taper * taper * (1.0 + 4.0 * ratio)
    return sill_factor / taper_radius * matern * taper * left_alive[:, None] * right_alive[None, :]

def add_block(accum, term, where):
    current = lax.dynamic_index_in_dim(accum, where, 1, keepdims=False)
    return lax.dynamic_update_index_in_dim(accum, current + term, where, 1)

def pair_terms(accum, entry, probes, blocks, alive, taper_radius):
    row_block = entry[0].astype(jnp.int32)
    col_block = entry[1].astype(jnp.int32)
    weight = entry[2].astype(jnp.float32)
    left = lax.dynamic_index_in_dim(blocks, row_block, 1, keepdims=False)
    right = lax.dynamic_index_in_dim(blocks, col_block, 1, keepdims=False)
    left_alive = lax.dynamic_index_in_dim(alive, row_block, 0, keepdims=False)
    right_alive = lax.dynamic_index_in_dim(alive, col_block, 0, keepdims=False)
    kernel = cov_tile(left, right, left_alive, right_alive, taper_radius)
    vec_col = lax.dynamic_index_in_dim(probes, col_block, 1, keepdims=False)
    vec_row = lax.dynamic_index_in_dim(probes, row_block, 1, keepdims=False)
    to_row = lax.dot_general(vec_col, kernel, (((1,), (1,)), ((), ())), precision=highest) * weight
    mirror = weight * (row_block != col_block).astype(jnp.float32)
    to_col = jnp.dot(vec_row, kernel, precision=highest) * mirror
    accum = add_block(accum, to_row, row_block)
    return add_block(accum, to_col, col_block)

def inner_products(first, second):
    return lax.dot_general(first, second, (((1,), (1,)), ((), ())), precision=highest)

def solve_small(matrix, rhs):
    factor = jnp.linalg.cholesky(matrix)
    return jax.scipy.linalg.cho_solve((factor, True), rhs)

def reference(right_side, coords, counts, pair_list):
    taper_radius = float(SPAN)
    alive = (lax.broadcasted_iota(jnp.int32, (NBLK, TILE), 1) < counts[:, None]).astype(jnp.float32)
    blocks = coords.reshape(3, NBLK, TILE)
    flat_alive = alive.reshape(NLOC)

    def apply_operator(direction):
        probes = direction.reshape(PROBES, NBLK, TILE)

        def scan_pair(accum, entry):
            return (pair_terms(accum, entry, probes, blocks, alive, taper_radius), None)
        accum, unused = lax.scan(scan_pair, jnp.zeros((PROBES, NBLK, TILE), jnp.float32), pair_list.T)
        return accum.reshape(PROBES, NLOC) + nugget * direction
    residual = right_side * flat_alive
    direction = residual
    solution = jnp.zeros_like(residual)
    norm_now = inner_products(residual, residual)
    for iteration in range(ITERS):
        image = apply_operator(direction)
        alpha = solve_small(inner_products(direction, image), norm_now)
        solution = solution + jnp.dot(alpha.T, direction, precision=highest)
        residual = residual - jnp.dot(alpha.T, image, precision=highest)
        if iteration + 1 < ITERS:
            norm_next = inner_products(residual, residual)
            beta = solve_small(norm_now, norm_next)
            direction = residual + jnp.dot(beta.T, direction, precision=highest)
            norm_now = norm_next
    return (solution, residual)
```

```python
import functools
import math

import jax
import jax.numpy as jnp
from jax import lax
from jax.experimental import pallas as pl
from jax.experimental.pallas import tpu as pltpu
from jax.sharding import PartitionSpec as P

SPAN = 4
BLOCKS = 4
SLOTS = 512
PROBES = 8
FAR = 5

sill = 0.1 / SPAN
nugget = 0.5
level = nugget + sill

KAPPA = math.sqrt(3.0) / (0.5 * SPAN) * math.log2(math.e)
REACH = SPAN * KAPPA
MATERN_ROOT = math.log2(math.e)
TAPER_ROOT = KAPPA * SPAN / 4.0
UNIT = REACH**4 * 2.0**REACH * MATERN_ROOT * TAPER_ROOT

PAIRS = [(i, j) for i in range(BLOCKS) for j in range(i + 1)]
CHUNK = 16
CHUNKS = SLOTS // CHUNK
XROW = 32

f32 = jnp.float32
bf16 = jnp.bfloat16
MESH = pl.DeviceIdType.MESH
HIGHEST = lax.Precision.HIGHEST
NT = (((1,), (1,)), ((), ()))


def split(x, parts):
    out = []
    for _ in range(parts - 1):
        piece = x.astype(bf16).astype(f32)
        out.append(piece)
        x = x - piece
    out.append(x.astype(bf16).astype(f32))
    return out


def two_parts(x):
    high = x.astype(bf16)
    low = (x - high.astype(f32)).astype(bf16)
    return jnp.concatenate([high, low], axis=0)


def mm(a, b):
    return jnp.dot(a, b, precision=HIGHEST, preferred_element_type=f32)


def inverse(matrix):
    rows = lax.broadcasted_iota(jnp.int32, (PROBES, PROBES), 0)
    eye = (rows == lax.broadcasted_iota(jnp.int32, (PROBES, PROBES), 1)).astype(f32)
    return eliminate(matrix, eye)


def eliminate(matrix, rhs):
    work = jnp.concatenate([matrix, rhs], axis=1)
    rows = lax.broadcasted_iota(jnp.int32, work.shape, 0)
    for k in range(PROBES):
        pivot = work[k : k + 1, k : k + 1]
        scaled = work[k : k + 1, :] / pivot
        column = jnp.broadcast_to(work[:, k : k + 1], work.shape)
        work = jnp.where(rows == k, scaled, work - column * scaled)
    return work[:, PROBES:]


def kernel(
    groups,
    plane,
    rs_ref,
    co_ref,
    cnt_ref,
    sol_ref,
    res_ref,
    cnt,
    co,
    geo_s,
    geo_r,
    qq,
    qc,
    alive,
    lraw,
    xc,
    lfeat,
    rraw,
    rfeat,
    xr,
    vrow,
    vcol,
    kc,
    yzs,
    tr,
    tc,
    mine,
    spill,
    other_in,
    spill_in,
    ahead_in,
    tile,
    sums_a,
    tile_b,
    sums_b,
    local_sem,
    geo_send,
    geo_recv,
    q_send,
    q_recv,
    mine_send,
    spill_send,
    other_recv,
    spill_recv,
    ahead_recv,
    red_send,
    red_recv,
):
    g = lax.axis_index("blk")
    c = lax.axis_index("rep")
    nxt = lax.rem(g + 1, groups)
    prv = lax.rem(g + groups - 1, groups)
    zs = groups // plane
    z, inplane = g // plane, lax.rem(g, plane)
    ring = zs * 2
    place = z * 2 + c

    def in_plane(k):
        return {"blk": z * plane + lax.rem(inplane + k, plane), "rep": c}

    def across(k):
        at = lax.rem(place + k, ring)
        return {"blk": (at // 2) * plane + inplane, "rep": lax.rem(at, 2)}

    barrier = pltpu.get_barrier_semaphore()

    def greet_plane(k, carry):
        pl.semaphore_signal(barrier, inc=1, device_id=in_plane(k), device_id_type=MESH)
        return carry

    def greet_across(k, carry):
        pl.semaphore_signal(barrier, inc=1, device_id=across(k), device_id_type=MESH)
        return carry

    for near in (prv, nxt):
        for core in (0, 1):
            pl.semaphore_signal(
                barrier, inc=1, device_id={"blk": near, "rep": core}, device_id_type=MESH
            )
    lax.fori_loop(1, plane, greet_plane, 0)
    lax.fori_loop(1, ring, greet_across, 0)

    loads = [
        pltpu.make_async_copy(cnt_ref, cnt, local_sem.at[0]),
        pltpu.make_async_copy(co_ref, co, local_sem.at[1]),
    ]
    for b in range(BLOCKS):
        loads.append(
            pltpu.make_async_copy(
                rs_ref.at[:, pl.ds(b * SLOTS, SLOTS)], qq.at[b, 0:PROBES], local_sem.at[2 + b]
            )
        )
    for load in loads:
        load.start()
    for load in loads:
        load.wait()

    slot = lax.broadcasted_iota(jnp.int32, (1, SLOTS), 1)
    for b in range(BLOCKS):
        live = (slot < cnt[b]).astype(f32)
        alive[0, b] = live
        geo_s[b // 2, (b % 2) * 4 : (b % 2) * 4 + 3] = co[:, b * SLOTS : (b + 1) * SLOTS]
        geo_s[b // 2, (b % 2) * 4 + 3 : (b % 2) * 4 + 4] = live
        qq[b, 0:PROBES] = qq[b, 0:PROBES] * live

    pl.semaphore_wait(barrier, 4 + plane - 1 + ring - 1)

    back = {"blk": prv, "rep": 1}
    geo_copy = pltpu.make_async_remote_copy(
        src_ref=geo_s.at[c],
        dst_ref=geo_r.at[c],
        send_sem=geo_send,
        recv_sem=geo_recv.at[c],
        device_id=back,
        device_id_type=MESH,
    )
    geo_copy.start()
    q_copies = []
    for h in range(2):
        copy = pltpu.make_async_remote_copy(
            src_ref=qq.at[2 * h + c, 0:PROBES],
            dst_ref=qc.at[2 * h + c, 0:PROBES],
            send_sem=q_send.at[h],
            recv_sem=q_recv.at[2 * h + c],
            device_id=back,
            device_id_type=MESH,
        )
        copy.start()
        q_copies.append(copy)

    origin = geo_s[0, 0:1, 0:1]

    def features(geo, b):
        r = (b % 2) * 4
        x = (geo[b // 2, r : r + 1] - origin) * KAPPA
        y = (geo[b // 2, r + 1 : r + 2] - 0.5) * KAPPA
        w = (geo[b // 2, r + 2 : r + 3] - 0.5) * KAPPA
        return x, split(y, 3), split(w, 3), split(y * y + w * w, 3)

    ones = jnp.ones((1, SLOTS), f32)
    lraw[...] = jnp.zeros_like(lraw)
    rraw[...] = jnp.zeros_like(rraw)
    for b in range(BLOCKS):
        x, ys, ws, ns = features(geo_s, b)
        rows = []
        for q in (ys, ws):
            rows += [-2.0 * q[k] for k in (0, 0, 1, 1, 0, 2)]
        rows += ns + [ones] * 3
        for k, row in enumerate(rows):
            lraw[b, k : k + 1] = row
        lraw[b, XROW : XROW + 1] = x
        turned = lraw[b].T
        xc[b] = turned
        lfeat[b] = turned.astype(bf16)
        vrow[b] = two_parts(qq[b, 0:PROBES])

    @pl.when(c == 0)
    def _():
        for h in range(2):
            geo_r[h] = geo_s[h]
        for b in range(BLOCKS):
            qc[b, 0:PROBES] = qq[b, 0:PROBES]

    @pl.when(c == 1)
    def _():
        for h in range(2):
            pltpu.make_async_copy(geo_s.at[h], geo_r.at[h], geo_recv.at[h]).wait()

    for b in range(BLOCKS):
        x, ys, ws, ns = features(geo_r, b)
        rows = []
        for q in (ys, ws):
            rows += [q[k] for k in (0, 1, 0, 1, 2, 0)]
        rows += [ones] * 3 + ns
        for k, row in enumerate(rows):
            rraw[b, k : k + 1] = row
        rfeat[b] = rraw[b].astype(bf16)
        xr[b] = x
        alive[1, b] = geo_r[b // 2, (b % 2) * 4 + 3 : (b % 2) * 4 + 4]

    def build(n, chunk):
        i, j = PAIRS[n]
        s = pl.ds(chunk * CHUNK, CHUNK)
        along = xc[i, s, XROW : XROW + 1] - xr[j]
        square = jnp.maximum(along * along + yzs[n % 2, s], 1e-12)
        dist = square * lax.rsqrt(square)
        inside = jnp.maximum(REACH - dist, 0.0)
        decay = jnp.exp2(inside)
        twice = inside * inside
        value = (twice * twice) * decay * ((dist + MATERN_ROOT) * (dist + TAPER_ROOT))
        high = value.astype(bf16)
        kc[n, s, 0:SLOTS] = high
        kc[n, s, SLOTS:] = (value - high.astype(f32)).astype(bf16)

    def across_part(n, quarter):
        i, j = PAIRS[n]
        s = pl.ds(quarter * 128, 128)
        yzs[n % 2, s] = jnp.dot(lfeat[i, s], rfeat[j], preferred_element_type=f32)

    mirror = jnp.where(c == 0, 0.0, 1.0).astype(f32)

    def apply(n, quarter, it):
        i, j = PAIRS[n]
        h = quarter % 2
        s = pl.ds(h * 256, 256)
        if quarter < 2:
            both = jnp.dot(vrow[i][:, h * 256 : h * 256 + 256], kc[n, s], preferred_element_type=f32)
            both = both[:, :SLOTS] + both[:, SLOTS:]
            part = both[:PROBES] + both[PROBES:]
            if i == j:
                part = part * mirror
            tc[it, j] += part
        else:
            both = lax.dot_general(vcol[j], kc[n, s, 0:SLOTS], NT, preferred_element_type=f32)
            both += lax.dot_general(vcol[j], kc[n, s, SLOTS:], NT, preferred_element_type=f32)
            tr[it, i, :, h * 256 : h * 256 + 256] += both[:PROBES] + both[PROBES:]

    tr[...] = jnp.zeros_like(tr)
    tc[...] = jnp.zeros_like(tc)

    sends = []

    def send_block(b, it):
        mine[it, b] = tr[it, b] + (1.0 - mirror) * tc[it, b]

        def copy(src, dst, send_sem, recv_sem, blk, rep):
            return pltpu.make_async_remote_copy(
                src_ref=src,
                dst_ref=dst,
                send_sem=send_sem,
                recv_sem=recv_sem,
                device_id={"blk": blk, "rep": rep},
                device_id_type=MESH,
            )

        first = copy(
            mine.at[it, b], other_in.at[it, b], mine_send.at[0, it, b], other_recv.at[it, b], g, 1 - c
        )
        first.start()
        sends.append(first)
        if it == 0:
            second = copy(
                mine.at[it, b], ahead_in.at[c, b], mine_send.at[1, it, b], ahead_recv.at[c, b], prv, 1
            )
            second.start()
            sends.append(second)

        @pl.when(c == 1)
        def _():
            for core in range(2):
                copy(
                    tc.at[it, b],
                    spill_in.at[it, b],
                    spill_send.at[core, it, b],
                    spill_recv.at[it, b],
                    nxt,
                    core,
                ).start()

    def wait_for(dst, sem):
        pltpu.make_async_copy(mine.at[0, 0], dst, sem).wait()

    def gather_block(b, it):
        wait_for(other_in.at[it, b], other_recv.at[it, b])
        wait_for(spill_in.at[it, b], spill_recv.at[it, b])
        total = (mine[it, b] + other_in[it, b]) + spill_in[it, b]
        old = qq[b, it * PROBES : (it + 1) * PROBES]
        qq[b, (it + 1) * PROBES : (it + 2) * PROBES] = total * (alive[0, b] * (1.0 / UNIT)) - old

    def gather_ahead(b):
        @pl.when(c == 0)
        def _():
            qc[b, PROBES:] = qq[b, PROBES : 2 * PROBES]

        @pl.when(c == 1)
        def _():
            for core in range(2):
                wait_for(ahead_in.at[core, b], ahead_recv.at[core, b])
            total = (ahead_in[0, b] + ahead_in[1, b]) + tc[0, b]
            qc[b, PROBES:] = total * (alive[1, b] * (1.0 / UNIT)) - qc[b, 0:PROBES]

    for quarter in range(4):
        across_part(0, quarter)

    @pl.when(c == 1)
    def _():
        for b in range(BLOCKS):
            wait_for(qc.at[b, 0:PROBES], q_recv.at[b])

    for b in range(BLOCKS):
        vcol[b] = two_parts(qc[b, 0:PROBES])

    last = len(PAIRS) - 1
    for n in range(len(PAIRS)):
        for chunk in range(CHUNKS):
            build(n, chunk)
            if chunk % 8 == 3 and n < last:
                across_part(n + 1, chunk // 8)
            if chunk % 8 == 7 and n > 0:
                apply(n - 1, chunk // 8, 0)
        if n > 0 and PAIRS[n - 1][0] == BLOCKS - 1:
            send_block(PAIRS[n - 1][1], 0)
    for quarter in range(4):
        apply(last, quarter, 0)
    send_block(BLOCKS - 1, 0)

    for n, (i, j) in enumerate(PAIRS):
        if j == 0:
            gather_block(i, 0)
            gather_ahead(i)
            vrow[i] = two_parts(qq[i, PROBES : 2 * PROBES])
            vcol[i] = two_parts(qc[i, PROBES:])
        for quarter in range(4):
            apply(n, quarter, 1)
        if i == BLOCKS - 1:
            send_block(j, 1)

    tile[...] = jnp.zeros_like(tile)

    @pl.when(c == 0)
    def _():
        gram = jnp.zeros((2 * PROBES, 2 * PROBES), f32)
        for b in range(BLOCKS):
            pair = qq[b, 0 : 2 * PROBES]
            gram += lax.dot_general(pair, pair, NT, precision=HIGHEST, preferred_element_type=f32)
        tile[:, 0:16] = gram[0:PROBES]
        tile[:, 16:32] = gram[PROBES:]

    part = jnp.zeros((PROBES, PROBES), f32)
    for b in range(BLOCKS):
        part += lax.dot_general(
            qq[b, PROBES : 2 * PROBES], tr[1, b], NT, precision=HIGHEST, preferred_element_type=f32
        )
        part += lax.dot_general(
            qc[b, PROBES:], tc[1, b], NT, precision=HIGHEST, preferred_element_type=f32
        )
    tile[:, 32:40] = part * (1.0 / UNIT)

    def spread(src, dst, me, count, target, k):
        def send(step, carry):
            pltpu.make_async_remote_copy(
                src_ref=src,
                dst_ref=dst.at[me],
                send_sem=red_send.at[k],
                recv_sem=red_recv.at[k],
                device_id=target(step),
                device_id_type=MESH,
            ).start()
            return carry

        lax.fori_loop(1, count, send, 0)
        dst[me] = src[...]
        everything = dst.at[pl.ds(0, count - 1)]
        pltpu.make_async_copy(everything, everything, red_recv.at[k]).wait()
        total = dst[0]
        for at in range(1, count):
            total = total + dst[at]
        return total

    tile_b[...] = spread(tile, sums_a, inplane, plane, in_plane, 0)
    sums = spread(tile_b, sums_b, place, ring, across, 1)

    for b in range(BLOCKS):
        gather_block(b, 1)

    h00, h01, h11 = sums[:, 0:8], sums[:, 8:16], sums[:, 24:32]
    h12 = sums[:, 32:40] - h11
    curv_inv = inverse(level * h00 + sill * h01)
    alpha = mm(curv_inv, h00)
    m2 = mm(curv_inv, h01)
    m1 = mm(curv_inv, h11)
    alpha_t = mm(h00, curv_inv)
    w_t = sill * mm(h01, curv_inv)
    n_fwd = sill * (mm(h00, m1) - mm(h01, m2))
    n_t = sill * (mm(h11, alpha) - mm(h01, m2))
    beta = sill * mm(curv_inv, n_t)
    beta_t = sill * mm(n_fwd, curv_inv)
    new = mm(h00, beta)
    f_fwd = sill * m2 + beta
    f_t = w_t + beta_t
    curv = level * new - sill * mm(n_fwd, f_fwd)
    curv += sill**3 * mm(mm(alpha_t, h12) - mm(h01, m1), alpha)
    both = mm(new, eliminate(curv, jnp.concatenate([f_t, sill * alpha_t], axis=1)))
    x_t, y_t = both[:, :PROBES], both[:, PROBES:]
    zero = jnp.zeros((PROBES, PROBES), f32)
    top = jnp.concatenate([alpha_t + x_t, -y_t, zero], axis=1)
    low = jnp.concatenate(
        [w_t - level * x_t, level * y_t - sill * x_t - sill * alpha_t, sill * y_t], axis=1
    )
    weights = jnp.concatenate([top, low], axis=0)
    for b in range(BLOCKS):
        result = mm(weights, qq[b])
        sol_ref[:, b * SLOTS : (b + 1) * SLOTS] = result[:PROBES]
        res_ref[:, b * SLOTS : (b + 1) * SLOTS] = result[PROBES:]

    geo_copy.wait_send()
    for copy in q_copies:
        copy.wait_send()
    for copy in sends:
        copy.wait_send()

    @pl.when(c == 1)
    def _():
        for it in range(2):
            for b in range(BLOCKS):
                for core in range(2):
                    pltpu.make_async_copy(
                        tc.at[it, b], spill.at[b], spill_send.at[core, it, b]
                    ).wait()

    for k, (dst, count) in enumerate(((sums_a, plane), (sums_b, ring))):
        everything = dst.at[pl.ds(0, count - 1)]
        pltpu.make_async_copy(everything, everything, red_send.at[k]).wait()


def on_device(groups, plane, right_side, coords, counts, pair_list):
    del pair_list
    ring = groups // plane * 2
    block = (BLOCKS, PROBES, SLOTS)
    dma = pltpu.SemaphoreType.DMA
    width = right_side.shape[1]
    shape = jax.ShapeDtypeStruct((PROBES, width), f32)
    anywhere = pl.BlockSpec(memory_space=pl.ANY)
    vmem = pl.BlockSpec(memory_space=pltpu.VMEM)
    return pl.pallas_call(
        functools.partial(kernel, groups, plane),
        out_shape=(shape, shape),
        in_specs=[anywhere] * 3,
        out_specs=(vmem, vmem),
        scratch_shapes=[
            pltpu.SMEM((BLOCKS,), jnp.int32),
            pltpu.VMEM((3, width), f32),
            pltpu.VMEM((2, 8, SLOTS), f32),
            pltpu.VMEM((2, 8, SLOTS), f32),
            pltpu.VMEM((BLOCKS, 3 * PROBES, SLOTS), f32),
            pltpu.VMEM((BLOCKS, 2 * PROBES, SLOTS), f32),
            pltpu.VMEM((2, BLOCKS, 1, SLOTS), f32),
            pltpu.VMEM((BLOCKS, 128, SLOTS), f32),
            pltpu.VMEM((BLOCKS, SLOTS, 128), f32),
            pltpu.VMEM((BLOCKS, SLOTS, 128), bf16),
            pltpu.VMEM((BLOCKS, 128, SLOTS), f32),
            pltpu.VMEM((BLOCKS, 128, SLOTS), bf16),
            pltpu.VMEM((BLOCKS, 1, SLOTS), f32),
            pltpu.VMEM((BLOCKS, 2 * PROBES, SLOTS), bf16),
            pltpu.VMEM((BLOCKS, 2 * PROBES, SLOTS), bf16),
            pltpu.VMEM((len(PAIRS), SLOTS, 2 * SLOTS), bf16),
            pltpu.VMEM((2, SLOTS, SLOTS), f32),
            pltpu.VMEM((2,) + block, f32),
            pltpu.VMEM((2,) + block, f32),
            pltpu.VMEM((2,) + block, f32),
            pltpu.VMEM(block, f32),
            pltpu.VMEM((2,) + block, f32),
            pltpu.VMEM((2,) + block, f32),
            pltpu.VMEM((2,) + block, f32),
            pltpu.VMEM((8, 128), f32),
            pltpu.VMEM((plane, 8, 128), f32),
            pltpu.VMEM((8, 128), f32),
            pltpu.VMEM((ring, 8, 128), f32),
            dma((6,)),
            dma,
            dma((2,)),
            dma((2,)),
            dma((BLOCKS,)),
            dma((2, 2, BLOCKS)),
            dma((2, 2, BLOCKS)),
            dma((2, BLOCKS)),
            dma((2, BLOCKS)),
            dma((2, BLOCKS)),
            dma((2,)),
            dma((2,)),
        ],
        compiler_params=pltpu.CompilerParams(
            collective_id=0, has_side_effects=True, vmem_limit_bytes=40 << 20
        ),
        name="block_cg",
    )(right_side, coords, counts)


def solution(mesh):
    groups = mesh.shape["blk"]
    plane = 16 if groups % 16 == 0 else 2
    placed = (P(None, "blk"), P(None, "blk"), P("blk"), P(None, ("blk", "rep")))
    return jax.shard_map(
        functools.partial(on_device, groups, plane),
        mesh=mesh,
        in_specs=placed,
        out_specs=(P(None, "blk"), P(None, "blk")),
        check_vma=False,
    )
```

```python
import functools
import math

import jax
import jax.numpy as jnp
from jax import lax
from jax.experimental import pallas as pl
from jax.experimental.pallas import tpu as pltpu
from jax.sharding import PartitionSpec as P

SPAN = 4
BLOCKS = 4
SLOTS = 512
PROBES = 8
FAR = 5

sill = 0.1 / SPAN
nugget = 0.5
level = nugget + sill

KAPPA = math.sqrt(3.0) / (0.5 * SPAN) * math.log2(math.e)
REACH = SPAN * KAPPA
MATERN_ROOT = math.log2(math.e)
TAPER_ROOT = KAPPA * SPAN / 4.0
UNIT = REACH**4 * 2.0**REACH * MATERN_ROOT * TAPER_ROOT

ROWS = ((3, 0), (3, 0), (2, 0), (1, 1), (0, 1))
COLS = ((3, -1), (0, 1), (0, 2), (0, 1), (0, 1))
KEPT = ((1, 0), (0, 0), (0, 1), (0, 0), (0, 0))
ORDER = (0, 1, 5, 6, 7, 8, 9, 2, 3, 4)
CHUNK = 16
CHUNKS = SLOTS // CHUNK
XROW = 32

f32 = jnp.float32
bf16 = jnp.bfloat16
MESH = pl.DeviceIdType.MESH
HIGHEST = lax.Precision.HIGHEST
NT = (((1,), (1,)), ((), ()))


def split(x, parts):
    out = []
    for _ in range(parts - 1):
        piece = x.astype(bf16).astype(f32)
        out.append(piece)
        x = x - piece
    out.append(x.astype(bf16).astype(f32))
    return out


def two_parts(x):
    high = x.astype(bf16)
    low = (x - high.astype(f32)).astype(bf16)
    return jnp.concatenate([high, low], axis=0)


def mm(a, b):
    return jnp.dot(a, b, precision=HIGHEST, preferred_element_type=f32)


def inverse(matrix):
    rows = lax.broadcasted_iota(jnp.int32, (PROBES, PROBES), 0)
    eye = (rows == lax.broadcasted_iota(jnp.int32, (PROBES, PROBES), 1)).astype(f32)
    return eliminate(matrix, eye)


def eliminate(matrix, rhs):
    work = jnp.concatenate([matrix, rhs], axis=1)
    rows = lax.broadcasted_iota(jnp.int32, work.shape, 0)
    for k in range(PROBES):
        pivot = work[k : k + 1, k : k + 1]
        scaled = work[k : k + 1, :] / pivot
        column = jnp.broadcast_to(work[:, k : k + 1], work.shape)
        work = jnp.where(rows == k, scaled, work - column * scaled)
    return work[:, PROBES:]


def kernel(
    groups,
    plane,
    rs_ref,
    co_ref,
    cnt_ref,
    sol_ref,
    res_ref,
    cnt,
    co,
    geo_s,
    geo_r,
    qq,
    qn,
    alive,
    lraw,
    xc,
    lfeat,
    rraw,
    rfeat,
    xr,
    vrow,
    vnext,
    kc,
    yzs,
    tr,
    tc,
    other_in,
    spill_in,
    ahead_in,
    tile,
    sums,
    rhs,
    local_sem,
    geo_send,
    geo_recv,
    q_send,
    q_recv,
    mine_send,
    ahead_send,
    spill_send,
    other_recv,
    spill_recv,
    ahead_recv,
    red_send,
    red_recv,
):
    g = lax.axis_index("blk")
    c = lax.axis_index("rep")
    core = c.astype(f32)
    nxt = lax.rem(g + 1, groups)
    prv = lax.rem(g + groups - 1, groups)
    zs = groups // plane
    z, inplane = g // plane, lax.rem(g, plane)
    ring = zs * 2
    place = z * 2 + c

    def in_plane(k):
        return {"blk": z * plane + lax.rem(inplane + k, plane), "rep": c}

    def across(k):
        at = lax.rem(place + k, ring)
        return {"blk": (at // 2) * plane + inplane, "rep": lax.rem(at, 2)}

    def column(k):
        return c if k == 0 else 3 - c

    loads = [
        pltpu.make_async_copy(co_ref, co, local_sem.at[1]),
        pltpu.make_async_copy(cnt_ref, cnt, local_sem.at[0]),
    ]
    for b in range(BLOCKS):
        loads.append(
            pltpu.make_async_copy(
                rs_ref.at[:, pl.ds(b * SLOTS, SLOTS)], qq.at[b, 0:PROBES], local_sem.at[2 + b]
            )
        )
    for load in loads:
        load.start()

    barrier = pltpu.get_barrier_semaphore()

    def greet_plane(k, carry):
        pl.semaphore_signal(barrier, inc=1, device_id=in_plane(k), device_id_type=MESH)
        return carry

    def greet_across(k, carry):
        pl.semaphore_signal(barrier, inc=1, device_id=across(k), device_id_type=MESH)
        return carry

    for near in (prv, nxt):
        for side in (0, 1):
            pl.semaphore_signal(
                barrier, inc=1, device_id={"blk": near, "rep": side}, device_id_type=MESH
            )
    lax.fori_loop(1, ring, greet_across, 0)
    lax.fori_loop(1, plane, greet_plane, 0)

    for load in loads:
        load.wait()

    slot = lax.broadcasted_iota(jnp.int32, (1, SLOTS), 1)
    for b in range(BLOCKS):
        live = (slot < cnt[b]).astype(f32)
        alive[b] = live
        geo_s[b, 0:3] = co[:, b * SLOTS : (b + 1) * SLOTS]
        geo_s[b, 3:4] = live
        qq[b, 0:PROBES] = qq[b, 0:PROBES] * live

    pl.semaphore_wait(barrier, 4 + plane - 1 + ring - 1)

    def remote(src, dst, send_sem, recv_sem, blk, rep):
        return pltpu.make_async_remote_copy(
            src_ref=src,
            dst_ref=dst,
            send_sem=send_sem,
            recv_sem=recv_sem,
            device_id={"blk": blk, "rep": rep},
            device_id_type=MESH,
        )

    sends = []

    def send(*args):
        copy = remote(*args)
        copy.start()
        sends.append(copy)

    for k in range(2):
        at = column(k)
        send(geo_s.at[at, 0:4], geo_r.at[k, 0:4], geo_send.at[k], geo_recv.at[k], prv, c)
    for k in range(2):
        at = column(k)
        send(qq.at[at, 0:PROBES], qn.at[k, 0:PROBES], q_send.at[k], q_recv.at[k], prv, c)

    origin = geo_s[0, 0:1, 0:1]
    ones = jnp.ones((1, SLOTS), f32)

    def features(geo):
        x = (geo[0:1] - origin) * KAPPA
        y = (geo[1:2] - 0.5) * KAPPA
        w = (geo[2:3] - 0.5) * KAPPA
        return x, split(y, 3), split(w, 3), split(y * y + w * w, 3)

    def row_features(b):
        x, ys, ws, ns = features(geo_s[b])
        rows = []
        for q in (ys, ws):
            rows += [-2.0 * q[k] for k in (0, 0, 1, 1, 0, 2)]
        rows += ns + [ones] * 3
        for k, row in enumerate(rows):
            lraw[b, k : k + 1] = row
        lraw[b, XROW : XROW + 1] = x
        turned = lraw[b].T
        xc[b] = turned
        lfeat[b] = turned.astype(bf16)

    def column_features(geo, at):
        x, ys, ws, ns = features(geo)
        rows = []
        for q in (ys, ws):
            rows += [q[k] for k in (0, 1, 0, 1, 2, 0)]
        rows += [ones] * 3 + ns
        for k, row in enumerate(rows):
            rraw[at, k : k + 1] = row
        rfeat[at] = rraw[at].astype(bf16)
        xr[at] = x

    lraw[...] = jnp.zeros_like(lraw)
    rraw[...] = jnp.zeros_like(rraw)
    for k in range(2):
        column_features(geo_s[column(k)], k)
    for b in reversed(range(BLOCKS)):
        row_features(b)
        vrow[b] = two_parts(qq[b, 0:PROBES])

    def pick(table, n):
        low, step = table[n % 5]
        return low + step * c if step else low

    def kept(n):
        return pick(KEPT, n) + 2 * (n // 5)

    def build(n, chunk, half):
        s = pl.ds(chunk * CHUNK, CHUNK)
        along = xc[pick(ROWS, n), s, XROW : XROW + 1] - xr[kept(n)]
        square = jnp.maximum(along * along + yzs[half, s], 1e-12)
        dist = square * lax.rsqrt(square)
        inside = jnp.maximum(REACH - dist, 0.0)
        decay = jnp.exp2(inside)
        twice = inside * inside
        value = (twice * twice) * decay * ((dist + MATERN_ROOT) * (dist + TAPER_ROOT))
        high = value.astype(bf16)
        kc[n, s, 0:SLOTS] = high
        kc[n, s, SLOTS:] = (value - high.astype(f32)).astype(bf16)

    def across_part(n, quarter, half):
        s = pl.ds(quarter * 128, 128)
        yzs[half, s] = jnp.dot(
            lfeat[pick(ROWS, n), s], rfeat[kept(n)], preferred_element_type=f32
        )

    mirrored = {0: core, 2: 1.0 - core, 4: 0.0 * core}

    def apply(n, quarter, it):
        i = pick(ROWS, n)
        h = quarter % 2
        s = pl.ds(h * 256, 256)
        if quarter < 2:
            both = jnp.dot(
                vrow[i, :, h * 256 : h * 256 + 256], kc[n, s], preferred_element_type=f32
            )
            both = both[:, :SLOTS] + both[:, SLOTS:]
            part = both[:PROBES] + both[PROBES:]
            if n in mirrored:
                part = part * mirrored[n]
            if n < 5:
                tr[it, pick(COLS, n)] += part
            else:
                tc[it, pick(KEPT, n)] += part
        else:
            vec = vrow[pick(COLS, n)] if n < 5 else vnext[pick(KEPT, n)]
            both = lax.dot_general(vec, kc[n, s, 0:SLOTS], NT, preferred_element_type=f32)
            both += lax.dot_general(vec, kc[n, s, SLOTS:], NT, preferred_element_type=f32)
            tr[it, i, :, h * 256 : h * 256 + 256] += both[:PROBES] + both[PROBES:]

    tr[...] = jnp.zeros_like(tr)
    tc[...] = jnp.zeros_like(tc)

    def send_rows(b, it):
        send(tr.at[it, b], other_in.at[it, b], mine_send.at[it, b], other_recv.at[it, b], g, 1 - c)
        if it == 0:
            k, user = {0: (0, 0), 3: (1, 0), 1: (0, 1), 2: (1, 1)}[b]
            send(tr.at[it, b], ahead_in.at[c, k], ahead_send.at[b], ahead_recv.at[c, k], prv, user)

    def send_spill(k, it):
        at = column(k)
        for side in range(2):
            send(
                tc.at[it, k],
                spill_in.at[it, at],
                spill_send.at[side, it, k],
                spill_recv.at[it, at],
                nxt,
                side,
            )

    def wait_for(dst, sem):
        pltpu.make_async_copy(dst, dst, sem).wait()

    def gather_block(b, it):
        wait_for(other_in.at[it, b], other_recv.at[it, b])
        wait_for(spill_in.at[it, b], spill_recv.at[it, b])
        total = (tr[it, b] + other_in[it, b]) + spill_in[it, b]
        old = qq[b, it * PROBES : (it + 1) * PROBES]
        qq[b, (it + 1) * PROBES : (it + 2) * PROBES] = total * (alive[b] * (1.0 / UNIT)) - old

    def gather_ahead(k):
        for side in range(2):
            wait_for(ahead_in.at[side, k], ahead_recv.at[side, k])
        total = (ahead_in[0, k] + ahead_in[1, k]) + tc[0, k]
        qn[k, PROBES:] = total * (geo_r[k, 3:4] * (1.0 / UNIT)) - qn[k, 0:PROBES]

    for quarter in range(4):
        across_part(ORDER[0], quarter, 0)
    for at, n in enumerate(ORDER):
        then = ORDER[at + 1] if at + 1 < len(ORDER) else None
        if at == 1:
            for k in range(2):
                wait_for(geo_r.at[k, 0:4], geo_recv.at[k])
                column_features(geo_r[k], 2 + k)
        if at == 2:
            for k in range(2):
                wait_for(qn.at[k, 0:PROBES], q_recv.at[k])
                vnext[k] = two_parts(qn[k, 0:PROBES])
        for chunk in range(CHUNKS):
            build(n, chunk, at % 2)
            if chunk % 8 == 3 and then is not None:
                across_part(then, chunk // 8, (at + 1) % 2)
            if chunk % 8 == 7 and at > 0:
                apply(ORDER[at - 1], chunk // 8, 0)
        if at == 4:
            send_rows(3, 0)
        if at == 5:
            send_spill(1, 0)
        if at == 7:
            send_spill(0, 0)
        if at == 9:
            send_rows(2, 0)
    for quarter in range(4):
        apply(ORDER[-1], quarter, 0)
    send_rows(1, 0)
    send_rows(0, 0)

    def ready(b):
        gather_block(b, 0)
        vrow[b] = two_parts(qq[b, PROBES : 2 * PROBES])

    def second(n):
        for quarter in range(4):
            apply(n, quarter, 1)

    ready(3)
    ready(2)
    second(0)
    ready(1)
    ready(0)
    for n in range(1, 5):
        second(n)

    def spread(turn, count, target):
        me = inplane if turn % 2 == 0 else place
        src, dst = tile.at[turn], sums.at[turn]

        def one(step, carry):
            pltpu.make_async_remote_copy(
                src_ref=src,
                dst_ref=dst.at[me],
                send_sem=red_send.at[turn],
                recv_sem=red_recv.at[turn],
                device_id=target(step),
                device_id_type=MESH,
            ).start()
            return carry

        lax.fori_loop(1, count, one, 0)
        dst[me] = src[...]

    def total_of(turn, count):
        everything = sums.at[turn, pl.ds(0, count - 1)]
        pltpu.make_async_copy(everything, everything, red_recv.at[turn]).wait()
        parts = [sums[turn, at] for at in range(count)]
        while len(parts) > 1:
            parts = [sum(parts[at : at + 2]) for at in range(0, len(parts), 2)]
        return parts[0]

    tile[...] = jnp.zeros_like(tile)
    gram = jnp.zeros((2 * PROBES, 2 * PROBES), f32)
    for b in range(2):
        pair = qq[2 * c + b, 0 : 2 * PROBES]
        gram += lax.dot_general(pair, pair, NT, precision=HIGHEST, preferred_element_type=f32)
    tile[0, :, 0:16] = gram[0:PROBES]
    tile[0, :, 16:32] = gram[PROBES:]
    spread(0, plane, in_plane)

    for k in range(2):
        gather_ahead(k)
        vnext[k] = two_parts(qn[k, PROBES:])
    for n in range(5, 10):
        second(n)

    part = jnp.zeros((PROBES, PROBES), f32)
    for b in range(BLOCKS):
        part += lax.dot_general(
            qq[b, PROBES : 2 * PROBES], tr[1, b], NT, precision=HIGHEST, preferred_element_type=f32
        )
    for k in range(2):
        part += lax.dot_general(
            qn[k, PROBES:], tc[1, k], NT, precision=HIGHEST, preferred_element_type=f32
        )
    tile[2, :, 0:8] = part * (1.0 / UNIT)
    spread(2, plane, in_plane)
    for k in range(2):
        send_spill(k, 1)
    for b in range(BLOCKS):
        send_rows(b, 1)

    tile[1] = total_of(0, plane)
    spread(1, ring, across)
    tile[3] = total_of(2, plane)
    spread(3, ring, across)
    early = total_of(1, ring)

    h00, h01, h11 = early[:, 0:8], early[:, 8:16], early[:, 24:32]
    curv_inv = inverse(level * h00 + sill * h01)
    alpha = mm(curv_inv, h00)
    m2 = mm(curv_inv, h01)
    m1 = mm(curv_inv, h11)
    alpha_t = mm(h00, curv_inv)
    w_t = sill * mm(h01, curv_inv)
    n_fwd = sill * (mm(h00, m1) - mm(h01, m2))
    n_t = sill * (mm(h11, alpha) - mm(h01, m2))
    beta = sill * mm(curv_inv, n_t)
    beta_t = sill * mm(n_fwd, curv_inv)
    new = mm(h00, beta)
    f_fwd = sill * m2 + beta
    f_t = w_t + beta_t
    known = level * new - sill * mm(n_fwd, f_fwd) - sill**3 * mm(mm(h01, m1), alpha)
    known -= sill**3 * mm(mm(alpha_t, h11), alpha)
    right = jnp.concatenate([f_t, sill * alpha_t], axis=1)
    zero = jnp.zeros((PROBES, PROBES), f32)
    first = jnp.concatenate(
        [
            jnp.concatenate([alpha_t, zero], axis=1),
            jnp.concatenate([w_t, -sill * alpha_t], axis=1),
        ],
        axis=0,
    )
    for b in range(BLOCKS):
        s = pl.ds(b * SLOTS, SLOTS)
        start = mm(first, qq[b, 0 : 2 * PROBES])
        sol_ref[:, s] = start[:PROBES]
        res_ref[:, s] = start[PROBES:]
        gather_block(b, 1)
        q0, q1, q2 = (qq[b, k * PROBES : (k + 1) * PROBES] for k in range(3))
        rhs[b, 0:PROBES, 0:SLOTS] = q0
        rhs[b, PROBES:, 0:SLOTS] = -q1
        rhs[b, 0:PROBES, SLOTS:] = -(level * q0 + sill * q1)
        rhs[b, PROBES:, SLOTS:] = level * q1 + sill * q2

    late = total_of(3, ring)
    curv = known + sill**3 * mm(mm(alpha_t, late[:, 0:8]), alpha)
    weights = mm(new, eliminate(curv, right))
    for b in range(BLOCKS):
        s = pl.ds(b * SLOTS, SLOTS)
        more = mm(weights, rhs[b])
        sol_ref[:, s] += more[:, :SLOTS]
        res_ref[:, s] += more[:, SLOTS:]

    for copy in sends:
        copy.wait_send()
    for turn in range(4):
        everything = sums.at[turn, pl.ds(0, (plane if turn % 2 == 0 else ring) - 1)]
        pltpu.make_async_copy(everything, everything, red_send.at[turn]).wait()


def on_device(groups, plane, right_side, coords, counts, pair_list):
    del pair_list
    ring = groups // plane * 2
    block = (BLOCKS, PROBES, SLOTS)
    dma = pltpu.SemaphoreType.DMA
    width = right_side.shape[1]
    shape = jax.ShapeDtypeStruct((PROBES, width), f32)
    anywhere = pl.BlockSpec(memory_space=pl.ANY)
    vmem = pl.BlockSpec(memory_space=pltpu.VMEM)
    return pl.pallas_call(
        functools.partial(kernel, groups, plane),
        out_shape=(shape, shape),
        in_specs=[anywhere] * 3,
        out_specs=(vmem, vmem),
        scratch_shapes=[
            pltpu.SMEM((BLOCKS,), jnp.int32),
            pltpu.VMEM((3, width), f32),
            pltpu.VMEM(block, f32),
            pltpu.VMEM((2, PROBES, SLOTS), f32),
            pltpu.VMEM((BLOCKS, 3 * PROBES, SLOTS), f32),
            pltpu.VMEM((2, 2 * PROBES, SLOTS), f32),
            pltpu.VMEM((BLOCKS, 1, SLOTS), f32),
            pltpu.VMEM((BLOCKS, 128, SLOTS), f32),
            pltpu.VMEM((BLOCKS, SLOTS, 128), f32),
            pltpu.VMEM((BLOCKS, SLOTS, 128), bf16),
            pltpu.VMEM((BLOCKS, 128, SLOTS), f32),
            pltpu.VMEM((BLOCKS, 128, SLOTS), bf16),
            pltpu.VMEM((BLOCKS, 1, SLOTS), f32),
            pltpu.VMEM((BLOCKS, 2 * PROBES, SLOTS), bf16),
            pltpu.VMEM((2, 2 * PROBES, SLOTS), bf16),
            pltpu.VMEM((len(ORDER), SLOTS, 2 * SLOTS), bf16),
            pltpu.VMEM((2, SLOTS, SLOTS), f32),
            pltpu.VMEM((2,) + block, f32),
            pltpu.VMEM((2, 2, PROBES, SLOTS), f32),
            pltpu.VMEM((2,) + block, f32),
            pltpu.VMEM((2,) + block, f32),
            pltpu.VMEM((2, 2, PROBES, SLOTS), f32),
            pltpu.VMEM((4, 8, 128), f32),
            pltpu.VMEM((4, max(plane, ring), 8, 128), f32),
            pltpu.VMEM((BLOCKS, 2 * PROBES, 2 * SLOTS), f32),
            dma((6,)),
            dma((2,)),
            dma((2,)),
            dma((2,)),
            dma((2,)),
            dma((2, BLOCKS)),
            dma((BLOCKS,)),
            dma((2, 2, 2)),
            dma((2, BLOCKS)),
            dma((2, BLOCKS)),
            dma((2, 2)),
            dma((4,)),
            dma((4,)),
        ],
        compiler_params=pltpu.CompilerParams(
            collective_id=0, has_side_effects=True, vmem_limit_bytes=60 << 20
        ),
        name="block_cg",
    )(right_side, coords, counts)


def solution(mesh):
    groups = mesh.shape["blk"]
    plane = 16 if groups % 16 == 0 else 2
    placed = (P(None, "blk"), P(None, "blk"), P("blk"), P(None, ("blk", "rep")))
    return jax.shard_map(
        functools.partial(on_device, groups, plane),
        mesh=mesh,
        in_specs=placed,
        out_specs=(P(None, "blk"), P(None, "blk")),
        check_vma=False,
    )
```

```python
import functools
import math

import jax
import jax.numpy as jnp
from jax import lax
from jax.experimental import pallas as pl
from jax.experimental.pallas import tpu as pltpu
from jax.sharding import PartitionSpec as P

SPAN = 4
BLOCKS = 4
SLOTS = 512
PROBES = 8
FAR = 5

sill = 0.1 / SPAN
nugget = 0.5
level = nugget + sill

KAPPA = math.sqrt(3.0) / (0.5 * SPAN)
REACH = SPAN * KAPPA
MATERN_ROOT = 1.0
TAPER_ROOT = KAPPA * SPAN / 4.0
UNIT = REACH**4 * math.exp(REACH) * MATERN_ROOT * TAPER_ROOT

ROWS = ((3, -1), (3, 0), (2, 1), (1, 1), (0, 1))
COLS = ((3, -1), (0, 2), (0, 1), (0, 1), (0, 1))
KEPT = ((1, 0), (0, 1), (0, 0), (0, 0), (0, 0))
DIAGONAL = (0, 4)
ORDER = (0, 1, 5, 6, 7, 8, 9, 2, 3, 4)
CHUNK = 16
CHUNKS = SLOTS // CHUNK
XROW = 32

f32 = jnp.float32
bf16 = jnp.bfloat16
MESH = pl.DeviceIdType.MESH
HIGHEST = lax.Precision.HIGHEST
NT = (((1,), (1,)), ((), ()))


def split(x, parts):
    out = []
    for _ in range(parts - 1):
        piece = x.astype(bf16).astype(f32)
        out.append(piece)
        x = x - piece
    out.append(x.astype(bf16).astype(f32))
    return out


def two_parts(x):
    high = x.astype(bf16)
    low = (x - high.astype(f32)).astype(bf16)
    return jnp.concatenate([high, low], axis=0)


def mm(a, b):
    terms = [a[:, k : k + 1] * b[k : k + 1] for k in range(PROBES)]
    while len(terms) > 1:
        terms = [functools.reduce(jnp.add, terms[at : at + 2]) for at in range(0, len(terms), 2)]
    return terms[0]


def inverse(matrix):
    rows = lax.broadcasted_iota(jnp.int32, (PROBES, PROBES), 0)
    eye = (rows == lax.broadcasted_iota(jnp.int32, (PROBES, PROBES), 1)).astype(f32)
    return eliminate(matrix, eye)


def eliminate(matrix, rhs):
    work = jnp.concatenate([matrix, rhs], axis=1)
    rows = lax.broadcasted_iota(jnp.int32, work.shape, 0)
    for k in range(PROBES):
        pivot = work[k : k + 1, k : k + 1]
        scaled = work[k : k + 1, :] / pivot
        column = jnp.broadcast_to(work[:, k : k + 1], work.shape)
        work = jnp.where(rows == k, scaled, work - column * scaled)
    return work[:, PROBES:]


def kernel(
    groups,
    plane,
    rs_ref,
    co_ref,
    cnt_ref,
    out_ref,
    cnt,
    co,
    geo_s,
    geo_r,
    qq,
    qn,
    alive,
    lraw,
    xc,
    lfeat,
    rraw,
    rfeat,
    xr,
    vrow,
    vnext,
    kc,
    yzs,
    tr,
    tc,
    other_in,
    spill_in,
    ahead_in,
    tile,
    sums,
    rhs,
    local_sem,
    geo_send,
    geo_recv,
    q_send,
    q_recv,
    mine_send,
    ahead_send,
    spill_send,
    other_recv,
    spill_recv,
    ahead_recv,
    red_send,
    red_recv,
):
    g = lax.axis_index("blk")
    c = lax.axis_index("rep")
    nxt = lax.rem(g + 1, groups)
    prv = lax.rem(g + groups - 1, groups)
    zs = groups // plane
    z, inplane = g // plane, lax.rem(g, plane)
    ring = zs * 2
    place = z * 2 + c

    def in_plane(k):
        return {"blk": z * plane + lax.rem(inplane + k, plane), "rep": c}

    def across(k):
        at = lax.rem(place + k, ring)
        return {"blk": (at // 2) * plane + inplane, "rep": lax.rem(at, 2)}

    def column(k):
        return c if k == 0 else 3 - c

    loads = [
        pltpu.make_async_copy(co_ref, co, local_sem.at[1]),
        pltpu.make_async_copy(cnt_ref, cnt, local_sem.at[0]),
    ]
    for b in range(BLOCKS):
        loads.append(
            pltpu.make_async_copy(
                rs_ref.at[:, pl.ds(b * SLOTS, SLOTS)], qq.at[b, 0:PROBES], local_sem.at[2 + b]
            )
        )
    for load in loads:
        load.start()

    barrier = pltpu.get_barrier_semaphore()

    def greet_plane(k, carry):
        pl.semaphore_signal(barrier, inc=1, device_id=in_plane(k), device_id_type=MESH)
        return carry

    def greet_across(k, carry):
        pl.semaphore_signal(barrier, inc=1, device_id=across(k), device_id_type=MESH)
        return carry

    for near in (prv, nxt):
        for side in (0, 1):
            pl.semaphore_signal(
                barrier, inc=1, device_id={"blk": near, "rep": side}, device_id_type=MESH
            )
    lax.fori_loop(1, ring, greet_across, 0)
    lax.fori_loop(1, plane, greet_plane, 0)

    for load in loads:
        load.wait()

    slot = lax.broadcasted_iota(jnp.int32, (1, SLOTS), 1)
    for b in range(BLOCKS):
        live = (slot < cnt[b]).astype(f32)
        alive[b] = live
        geo_s[b, 0:3] = co[:, b * SLOTS : (b + 1) * SLOTS]
        geo_s[b, 3:4] = live
        qq[b, 0:PROBES] = qq[b, 0:PROBES] * live

    pl.semaphore_wait(barrier, 4 + plane - 1 + ring - 1)

    def remote(src, dst, send_sem, recv_sem, blk, rep):
        return pltpu.make_async_remote_copy(
            src_ref=src,
            dst_ref=dst,
            send_sem=send_sem,
            recv_sem=recv_sem,
            device_id={"blk": blk, "rep": rep},
            device_id_type=MESH,
        )

    sends = []

    def send(*args):
        copy = remote(*args)
        copy.start()
        sends.append(copy)

    for k in range(2):
        at = column(k)
        send(geo_s.at[at, 0:4], geo_r.at[k, 0:4], geo_send.at[k], geo_recv.at[k], prv, c)
    for k in range(2):
        at = column(k)
        send(qq.at[at, 0:PROBES], qn.at[k, 0:PROBES], q_send.at[k], q_recv.at[k], prv, c)

    origin = geo_s[0, 0:1, 0:1]
    ones = jnp.ones((1, SLOTS), f32)

    def features(geo):
        x = (geo[0:1] - origin) * KAPPA
        y = (geo[1:2] - 0.5) * KAPPA
        w = (geo[2:3] - 0.5) * KAPPA
        return x, split(y, 3), split(w, 3), split(y * y + w * w, 3)

    def row_features(b):
        x, ys, ws, ns = features(geo_s[b])
        rows = []
        for q in (ys, ws):
            rows += [-2.0 * q[k] for k in (0, 0, 1, 1, 0, 2)]
        rows += ns + [ones] * 3
        for k, row in enumerate(rows):
            lraw[b, k : k + 1] = row
        lraw[b, XROW : XROW + 1] = x
        turned = lraw[b].T
        xc[b] = turned
        lfeat[b] = turned.astype(bf16)

    def column_features(geo, at):
        x, ys, ws, ns = features(geo)
        rows = []
        for q in (ys, ws):
            rows += [q[k] for k in (0, 1, 0, 1, 2, 0)]
        rows += [ones] * 3 + ns
        for k, row in enumerate(rows):
            rraw[at, k : k + 1] = row
        rfeat[at] = rraw[at].astype(bf16)
        xr[at] = x

    lraw[...] = jnp.zeros_like(lraw)
    rraw[...] = jnp.zeros_like(rraw)
    for k in range(2):
        column_features(geo_s[column(k)], k)
    for b in reversed(range(BLOCKS)):
        row_features(b)
        vrow[b] = two_parts(qq[b, 0:PROBES])

    def pick(table, n):
        low, step = table[n % 5]
        return low + step * c if step else low

    def kept(n):
        return pick(KEPT, n) + 2 * (n // 5)

    def build(n, chunk, half):
        s = pl.ds(chunk * CHUNK, CHUNK)
        along = xc[pick(ROWS, n), s, XROW : XROW + 1] - xr[kept(n)]
        square = jnp.maximum(along * along + yzs[half, s], 1e-12)
        dist = square * lax.rsqrt(square)
        inside = jnp.maximum(REACH - dist, 0.0)
        decay = jnp.exp(inside)
        twice = inside * inside
        value = (twice * twice) * decay * ((dist + MATERN_ROOT) * (dist + TAPER_ROOT))
        high = value.astype(bf16)
        kc[n, s, 0:SLOTS] = high
        kc[n, s, SLOTS:] = (value - high.astype(f32)).astype(bf16)

    def across_part(n, quarter, half):
        s = pl.ds(quarter * 128, 128)
        yzs[half, s] = jnp.dot(
            lfeat[pick(ROWS, n), s], rfeat[kept(n)], preferred_element_type=f32
        )

    def apply(n, quarter, it):
        i = pick(ROWS, n)
        h = quarter % 2
        s = pl.ds(h * 256, 256)
        if quarter < 2 and n in DIAGONAL:
            return
        if quarter < 2:
            both = jnp.dot(
                vrow[i, :, h * 256 : h * 256 + 256], kc[n, s], preferred_element_type=f32
            )
            both = both[:, :SLOTS] + both[:, SLOTS:]
            part = both[:PROBES] + both[PROBES:]
            if n < 5:
                tr[it, pick(COLS, n)] += part
            else:
                tc[it, pick(KEPT, n)] += part
        else:
            vec = vrow[pick(COLS, n)] if n < 5 else vnext[pick(KEPT, n)]
            both = lax.dot_general(vec, kc[n, s, 0:SLOTS], NT, preferred_element_type=f32)
            both += lax.dot_general(vec, kc[n, s, SLOTS:], NT, preferred_element_type=f32)
            tr[it, i, :, h * 256 : h * 256 + 256] += both[:PROBES] + both[PROBES:]

    tr[...] = jnp.zeros_like(tr)
    tc[...] = jnp.zeros_like(tc)

    def send_rows(b, it):
        send(tr.at[it, b], other_in.at[it, b], mine_send.at[it, b], other_recv.at[it, b], g, 1 - c)
        if it == 0:
            k, user = {0: (0, 0), 3: (1, 0), 1: (0, 1), 2: (1, 1)}[b]
            send(tr.at[it, b], ahead_in.at[c, k], ahead_send.at[b], ahead_recv.at[c, k], prv, user)

    def send_spill(k, it):
        at = column(k)
        for side in range(2):
            send(
                tc.at[it, k],
                spill_in.at[it, at],
                spill_send.at[side, it, k],
                spill_recv.at[it, at],
                nxt,
                side,
            )

    def wait_for(dst, sem):
        pltpu.make_async_copy(dst, dst, sem).wait()

    def gather_block(b, it):
        wait_for(other_in.at[it, b], other_recv.at[it, b])
        wait_for(spill_in.at[it, b], spill_recv.at[it, b])
        total = (tr[it, b] + other_in[it, b]) + spill_in[it, b]
        old = qq[b, it * PROBES : (it + 1) * PROBES]
        qq[b, (it + 1) * PROBES : (it + 2) * PROBES] = total * (alive[b] * (1.0 / UNIT)) - old

    def gather_ahead(k):
        for side in range(2):
            wait_for(ahead_in.at[side, k], ahead_recv.at[side, k])
        total = (ahead_in[0, k] + ahead_in[1, k]) + tc[0, k]
        qn[k, PROBES:] = total * (geo_r[k, 3:4] * (1.0 / UNIT)) - qn[k, 0:PROBES]

    for quarter in range(4):
        across_part(ORDER[0], quarter, 0)
    for at, n in enumerate(ORDER):
        then = ORDER[at + 1] if at + 1 < len(ORDER) else None
        if at == 2:
            for k in range(2):
                wait_for(qn.at[k, 0:PROBES], q_recv.at[k])
                vnext[k] = two_parts(qn[k, 0:PROBES])
        for chunk in range(CHUNKS):
            if at == 1 and chunk == CHUNKS // 2:
                for k in range(2):
                    wait_for(geo_r.at[k, 0:4], geo_recv.at[k])
                    column_features(geo_r[k], 2 + k)
            build(n, chunk, at % 2)
            if at == 1:
                if chunk >= CHUNKS // 2 and chunk % 4 == 1:
                    across_part(then, (chunk - CHUNKS // 2) // 4, (at + 1) % 2)
            elif chunk % 8 == 3 and then is not None:
                across_part(then, chunk // 8, (at + 1) % 2)
            if chunk % 8 == 7 and at > 0:
                apply(ORDER[at - 1], chunk // 8, 0)
        if at == 4:
            send_spill(1, 0)
        if at == 7:
            send_spill(0, 0)
        if at == 8:
            send_rows(3, 0)
        if at == 9:
            send_rows(2, 0)
    for quarter in range(4):
        apply(ORDER[-1], quarter, 0)
    send_rows(1, 0)
    send_rows(0, 0)

    def spread(turn, me, count, target):
        src, dst = tile.at[turn], sums.at[turn]

        def one(step, carry):
            pltpu.make_async_remote_copy(
                src_ref=src,
                dst_ref=dst.at[me],
                send_sem=red_send.at[turn],
                recv_sem=red_recv.at[turn],
                device_id=target(step),
                device_id_type=MESH,
            ).start()
            return carry

        lax.fori_loop(1, count, one, 0)
        dst[me] = src[...]

    def total_of(turn, count):
        everything = sums.at[turn, pl.ds(0, count - 1)]
        pltpu.make_async_copy(everything, everything, red_recv.at[turn]).wait()
        parts = [sums[turn, at] for at in range(count)]
        while len(parts) > 1:
            parts = [functools.reduce(jnp.add, parts[at : at + 2]) for at in range(0, len(parts), 2)]
        return parts[0]

    def ready(b):
        gather_block(b, 0)
        vrow[b] = two_parts(qq[b, PROBES : 2 * PROBES])

    def second(n):
        for quarter in range(4):
            apply(n, quarter, 1)

    ready(3)
    ready(2)
    second(0)
    ready(1)
    ready(0)

    for n in range(1, 5):
        second(n)

    tile[...] = jnp.zeros_like(tile)
    gram = jnp.zeros((2 * PROBES, 2 * PROBES), f32)
    for b in range(2):
        pair = qq[2 * c + b, 0 : 2 * PROBES]
        gram += lax.dot_general(pair, pair, NT, precision=HIGHEST, preferred_element_type=f32)
    tile[0, :, 0:16] = gram[0:PROBES]
    tile[0, :, 16:32] = gram[PROBES:]

    for k in range(2):
        gather_ahead(k)
        vnext[k] = two_parts(qn[k, PROBES:])
    for n in range(5, 10):
        second(n)

    part = jnp.zeros((PROBES, PROBES), f32)
    for b in range(BLOCKS):
        part += lax.dot_general(
            qq[b, PROBES : 2 * PROBES], tr[1, b], NT, precision=HIGHEST, preferred_element_type=f32
        )
    for k in range(2):
        part += lax.dot_general(
            qn[k, PROBES:], tc[1, k], NT, precision=HIGHEST, preferred_element_type=f32
        )
    tile[0, :, 32:40] = part * (1.0 / UNIT)
    spread(0, inplane, plane, in_plane)
    for k in range(2):
        send_spill(k, 1)
    for b in range(BLOCKS):
        send_rows(b, 1)
    tile[1] = total_of(0, plane)
    spread(1, place, ring, across)

    for b in range(BLOCKS):
        gather_block(b, 1)
        for k in range(3 * PROBES):
            rhs[b, k] = jnp.broadcast_to(qq[b, k : k + 1], (PROBES, SLOTS))

    totals = total_of(1, ring)
    h00, h01, h11 = totals[:, 0:8], totals[:, 8:16], totals[:, 24:32]
    curv_inv = inverse(level * h00 + sill * h01)
    left = mm(curv_inv, totals[:, 0:40])
    alpha, m2, m1, m12 = (left[:, at : at + PROBES] for at in (0, 8, 24, 32))
    alpha_t = mm(h00, curv_inv)
    w_t = sill * mm(h01, curv_inv)
    middle = mm(h01, m2)
    n_fwd = sill * (mm(h00, m1) - middle)
    n_t = sill * (mm(h11, alpha) - middle)
    beta = sill * mm(curv_inv, n_t)
    beta_t = sill * mm(n_fwd, curv_inv)
    new = mm(h00, beta)
    inner = mm(h00, m12 - m1) - mm(h01, m1)
    curv = level * new - sill * mm(n_fwd, sill * m2 + beta) + sill**3 * mm(inner, alpha)
    x_y = mm(new, eliminate(curv, jnp.concatenate([w_t + beta_t, sill * alpha_t], axis=1)))
    x_t, y_t = x_y[:, :PROBES], x_y[:, PROBES:]
    top = (alpha_t + x_t, -y_t)
    low = (w_t - level * x_t, level * y_t - sill * x_t - sill * alpha_t, sill * y_t)
    for h, weights in enumerate((top, low)):
        columns = [part[:, k : k + 1] for part in weights for k in range(PROBES)]
        for b in range(BLOCKS):
            terms = [column * rhs[b, k] for k, column in enumerate(columns)]
            while len(terms) > 1:
                terms = [functools.reduce(jnp.add, terms[at : at + 2]) for at in range(0, len(terms), 2)]
            out_ref[h * PROBES : (h + 1) * PROBES, b * SLOTS : (b + 1) * SLOTS] = terms[0]

    for copy in sends:
        copy.wait_send()
    for turn, count in enumerate((plane, ring)):
        everything = sums.at[turn, pl.ds(0, count - 1)]
        pltpu.make_async_copy(everything, everything, red_send.at[turn]).wait()


def on_device(groups, plane, right_side, coords, counts, pair_list):
    del pair_list
    ring = groups // plane * 2
    block = (BLOCKS, PROBES, SLOTS)
    dma = pltpu.SemaphoreType.DMA
    width = right_side.shape[1]
    shape = jax.ShapeDtypeStruct((2 * PROBES, width), f32)
    anywhere = pl.BlockSpec(memory_space=pl.ANY)
    vmem = pl.BlockSpec(memory_space=pltpu.VMEM)
    both = pl.pallas_call(
        functools.partial(kernel, groups, plane),
        out_shape=shape,
        in_specs=[anywhere] * 3,
        out_specs=vmem,
        scratch_shapes=[
            pltpu.SMEM((BLOCKS,), jnp.int32),
            pltpu.VMEM((3, width), f32),
            pltpu.VMEM(block, f32),
            pltpu.VMEM((2, PROBES, SLOTS), f32),
            pltpu.VMEM((BLOCKS, 3 * PROBES, SLOTS), f32),
            pltpu.VMEM((2, 2 * PROBES, SLOTS), f32),
            pltpu.VMEM((BLOCKS, 1, SLOTS), f32),
            pltpu.VMEM((BLOCKS, 128, SLOTS), f32),
            pltpu.VMEM((BLOCKS, SLOTS, 128), f32),
            pltpu.VMEM((BLOCKS, SLOTS, 128), bf16),
            pltpu.VMEM((BLOCKS, 128, SLOTS), f32),
            pltpu.VMEM((BLOCKS, 128, SLOTS), bf16),
            pltpu.VMEM((BLOCKS, 1, SLOTS), f32),
            pltpu.VMEM((BLOCKS, 2 * PROBES, SLOTS), bf16),
            pltpu.VMEM((2, 2 * PROBES, SLOTS), bf16),
            pltpu.VMEM((len(ORDER), SLOTS, 2 * SLOTS), bf16),
            pltpu.VMEM((2, SLOTS, SLOTS), f32),
            pltpu.VMEM((2,) + block, f32),
            pltpu.VMEM((2, 2, PROBES, SLOTS), f32),
            pltpu.VMEM((2,) + block, f32),
            pltpu.VMEM((2,) + block, f32),
            pltpu.VMEM((2, 2, PROBES, SLOTS), f32),
            pltpu.VMEM((2, 8, 128), f32),
            pltpu.VMEM((2, max(plane, ring), 8, 128), f32),
            pltpu.VMEM((BLOCKS, 3 * PROBES, PROBES, SLOTS), f32),
            dma((6,)),
            dma((2,)),
            dma((2,)),
            dma((2,)),
            dma((2,)),
            dma((2, BLOCKS)),
            dma((BLOCKS,)),
            dma((2, 2, 2)),
            dma((2, BLOCKS)),
            dma((2, BLOCKS)),
            dma((2, 2)),
            dma((2,)),
            dma((2,)),
        ],
        compiler_params=pltpu.CompilerParams(
            collective_id=0, has_side_effects=True, vmem_limit_bytes=60 << 20
        ),
        name="block_cg",
    )(right_side, coords, counts)
    return both[:PROBES], both[PROBES:]


def solution(mesh):
    groups = mesh.shape["blk"]
    plane = 16 if groups % 16 == 0 else 2
    placed = (P(None, "blk"), P(None, "blk"), P("blk"), P(None, ("blk", "rep")))
    return jax.shard_map(
        functools.partial(on_device, groups, plane),
        mesh=mesh,
        in_specs=placed,
        out_specs=(P(None, "blk"), P(None, "blk")),
        check_vma=False,
    )
```

```python
import functools
import math

import jax
import jax.numpy as jnp
from jax import lax
from jax.experimental import pallas as pl
from jax.experimental.pallas import tpu as pltpu
from jax.sharding import PartitionSpec as P

SPAN = 4
BLOCKS = 4
SLOTS = 512
PROBES = 8
FAR = 5

sill = 0.1 / SPAN
nugget = 0.5
level = nugget + sill

KAPPA = math.sqrt(3.0) / (0.5 * SPAN)
REACH = SPAN * KAPPA
MATERN_ROOT = 1.0
TAPER_ROOT = KAPPA * SPAN / 4.0
UNIT = REACH**4 * math.exp(REACH) * MATERN_ROOT * TAPER_ROOT

ROWS = ((3, -1), (3, 0), (2, 1), (1, 1), (0, 1))
COLS = ((3, -1), (0, 2), (0, 1), (0, 1), (0, 1))
KEPT = ((1, 0), (0, 1), (0, 0), (0, 0), (0, 0))
DIAGONAL = (0, 4)
SPILLED = ((0, 0), (1, 0), (1, 1), (0, 1))
ORDER = (0, 1, 5, 6, 7, 8, 9, 2, 3, 4)
CHUNK = 16
CHUNKS = SLOTS // CHUNK
XROW = 32

f32 = jnp.float32
bf16 = jnp.bfloat16
MESH = pl.DeviceIdType.MESH
NT = (((1,), (1,)), ((), ()))


def split(x, parts):
    out = []
    for _ in range(parts - 1):
        piece = x.astype(bf16).astype(f32)
        out.append(piece)
        x = x - piece
    out.append(x.astype(bf16).astype(f32))
    return out


def two_parts(x):
    high = x.astype(bf16)
    low = (x - high.astype(f32)).astype(bf16)
    return jnp.concatenate([high, low], axis=0)


def mm(a, b):
    terms = [a[:, k : k + 1] * b[k : k + 1] for k in range(PROBES)]
    while len(terms) > 1:
        terms = [functools.reduce(jnp.add, terms[at : at + 2]) for at in range(0, len(terms), 2)]
    return terms[0]


def inverse(matrix):
    rows = lax.broadcasted_iota(jnp.int32, (PROBES, PROBES), 0)
    eye = (rows == lax.broadcasted_iota(jnp.int32, (PROBES, PROBES), 1)).astype(f32)
    return eliminate(matrix, eye)


def eliminate(matrix, rhs):
    work = jnp.concatenate([matrix, rhs], axis=1)
    rows = lax.broadcasted_iota(jnp.int32, work.shape, 0)
    for k in range(PROBES):
        pivot = work[k : k + 1, k : k + 1]
        scaled = work[k : k + 1, :] / pivot
        column = jnp.broadcast_to(work[:, k : k + 1], work.shape)
        work = jnp.where(rows == k, scaled, work - column * scaled)
    return work[:, PROBES:]


def kernel(
    groups,
    plane,
    rs_ref,
    co_ref,
    cnt_ref,
    out_ref,
    cnt,
    co,
    geo_s,
    geo_out,
    geo_r,
    q_out,
    qq,
    qn,
    alive,
    lraw,
    xc,
    lfeat,
    rraw,
    rfeat,
    xr,
    vrow,
    vnext,
    kc,
    yzs,
    tr,
    tc,
    other_in,
    spill_in,
    ahead_in,
    tile,
    sums,
    rhs,
    local_sem,
    geo_send,
    geo_recv,
    q_send,
    q_recv,
    mine_send,
    ahead_send,
    spill_send,
    other_recv,
    spill_recv,
    ahead_recv,
    red_send,
    red_recv,
):
    g = lax.axis_index("blk")
    c = lax.axis_index("rep")
    nxt = lax.rem(g + 1, groups)
    prv = lax.rem(g + groups - 1, groups)
    zs = groups // plane
    z, inplane = g // plane, lax.rem(g, plane)
    ring = zs * 2
    place = z * 2 + c

    def in_plane(k):
        return {"blk": z * plane + lax.rem(inplane + k, plane), "rep": c}

    def along_z(k):
        return {"blk": lax.rem(z + k, zs) * plane + inplane, "rep": c}

    def across(k):
        at = lax.rem(place + k, ring)
        return {"blk": (at // 2) * plane + inplane, "rep": lax.rem(at, 2)}

    def column(k):
        return c if k == 0 else 3 - c

    loads = [
        pltpu.make_async_copy(co_ref, co, local_sem.at[1]),
        pltpu.make_async_copy(cnt_ref, cnt, local_sem.at[0]),
    ]
    for b in range(BLOCKS):
        loads.append(
            pltpu.make_async_copy(
                rs_ref.at[:, pl.ds(b * SLOTS, SLOTS)], qq.at[b, 0:PROBES], local_sem.at[2 + b]
            )
        )
    for load in loads:
        load.start()

    barrier = pltpu.get_barrier_semaphore()

    def greet_plane(k, carry):
        pl.semaphore_signal(barrier, inc=1, device_id=in_plane(k), device_id_type=MESH)
        return carry

    def greet_across(k, carry):
        pl.semaphore_signal(barrier, inc=1, device_id=across(k), device_id_type=MESH)
        return carry

    for near in (prv, nxt):
        for side in (0, 1):
            pl.semaphore_signal(
                barrier, inc=1, device_id={"blk": near, "rep": side}, device_id_type=MESH
            )
    lax.fori_loop(1, ring, greet_across, 0)
    lax.fori_loop(1, plane, greet_plane, 0)

    for load in loads:
        load.wait()

    slot = lax.broadcasted_iota(jnp.int32, (1, SLOTS), 1)
    for b in range(BLOCKS):
        live = (slot < cnt[b]).astype(f32)
        alive[b] = live
        geo_s[b, 0:3] = co[:, b * SLOTS : (b + 1) * SLOTS]
        geo_s[b, 3:4] = live
        qq[b, 0:PROBES] = qq[b, 0:PROBES] * live

    pl.semaphore_wait(barrier, 4 + plane - 1 + ring - 1)

    def remote(src, dst, send_sem, recv_sem, blk, rep):
        return pltpu.make_async_remote_copy(
            src_ref=src,
            dst_ref=dst,
            send_sem=send_sem,
            recv_sem=recv_sem,
            device_id={"blk": blk, "rep": rep},
            device_id_type=MESH,
        )

    sends = []

    def send(*args):
        copy = remote(*args)
        copy.start()
        sends.append(copy)

    for k in range(2):
        geo_out[4 * k : 4 * k + 4] = geo_s[column(k), 0:4]
        q_out[k] = qq[column(k), 0:PROBES]
    send(geo_out, geo_r, geo_send, geo_recv, prv, c)
    send(q_out, qn.at[0], q_send, q_recv, prv, c)

    origin = geo_s[0, 0:1, 0:1]
    ones = jnp.ones((1, SLOTS), f32)

    def features(geo):
        x = (geo[0:1] - origin) * KAPPA
        y = (geo[1:2] - 0.5) * KAPPA
        w = (geo[2:3] - 0.5) * KAPPA
        return x, split(y, 3), split(w, 3), split(y * y + w * w, 3)

    def row_features(b):
        x, ys, ws, ns = features(geo_s[b])
        rows = []
        for q in (ys, ws):
            rows += [-2.0 * q[k] for k in (0, 0, 1, 1, 0, 2)]
        rows += ns + [ones] * 3
        for k, row in enumerate(rows):
            lraw[b, k : k + 1] = row
        lraw[b, XROW : XROW + 1] = x
        turned = lraw[b].T
        xc[b] = turned
        lfeat[b] = turned.astype(bf16)

    def column_features(geo, at):
        x, ys, ws, ns = features(geo)
        rows = []
        for q in (ys, ws):
            rows += [q[k] for k in (0, 1, 0, 1, 2, 0)]
        rows += [ones] * 3 + ns
        for k, row in enumerate(rows):
            rraw[at, k : k + 1] = row
        rfeat[at] = rraw[at].astype(bf16)
        xr[at] = x

    lraw[...] = jnp.zeros_like(lraw)
    rraw[...] = jnp.zeros_like(rraw)
    for k in range(2):
        column_features(geo_s[column(k)], k)
    for b in reversed(range(BLOCKS)):
        row_features(b)
        vrow[b] = two_parts(qq[b, 0:PROBES])

    def pick(table, n):
        low, step = table[n % 5]
        return low + step * c if step else low

    def kept(n):
        return pick(KEPT, n) + 2 * (n // 5)

    def build(n, chunk, half):
        s = pl.ds(chunk * CHUNK, CHUNK)
        along = xc[pick(ROWS, n), s, XROW : XROW + 1] - xr[kept(n)]
        square = jnp.maximum(along * along + yzs[half, s], 1e-12)
        dist = square * lax.rsqrt(square)
        inside = jnp.maximum(REACH - dist, 0.0)
        decay = jnp.exp(inside)
        twice = inside * inside
        value = (twice * twice) * decay * ((dist + MATERN_ROOT) * (dist + TAPER_ROOT))
        high = value.astype(bf16)
        kc[n, s, 0:SLOTS] = high
        kc[n, s, SLOTS:] = (value - high.astype(f32)).astype(bf16)

    def across_part(n, quarter, half):
        s = pl.ds(quarter * 128, 128)
        yzs[half, s] = jnp.dot(
            lfeat[pick(ROWS, n), s], rfeat[kept(n)], preferred_element_type=f32
        )

    def apply(n, quarter, it):
        i = pick(ROWS, n)
        h = quarter % 2
        s = pl.ds(h * 256, 256)
        if quarter < 2 and n in DIAGONAL:
            return
        if quarter < 2:
            both = jnp.dot(
                vrow[i, :, h * 256 : h * 256 + 256], kc[n, s], preferred_element_type=f32
            )
            both = both[:, :SLOTS] + both[:, SLOTS:]
            part = both[:PROBES] + both[PROBES:]
            if n < 5:
                tr[it, pick(COLS, n)] += part
            else:
                tc[it, pick(KEPT, n)] += part
        else:
            vec = vrow[pick(COLS, n)] if n < 5 else vnext[pick(KEPT, n)]
            both = lax.dot_general(vec, kc[n, s, 0:SLOTS], NT, preferred_element_type=f32)
            both += lax.dot_general(vec, kc[n, s, SLOTS:], NT, preferred_element_type=f32)
            tr[it, i, :, h * 256 : h * 256 + 256] += both[:PROBES] + both[PROBES:]

    tr[...] = jnp.zeros_like(tr)
    tc[...] = jnp.zeros_like(tc)

    def send_rows(low, high, it):
        send(
            tr.at[it, low:high],
            other_in.at[it, low:high],
            mine_send.at[it, low],
            other_recv.at[it, low],
            g,
            1 - c,
        )

    def send_ahead(b):
        k, user = {0: (0, 0), 3: (1, 0), 1: (0, 1), 2: (1, 1)}[b]
        send(tr.at[0, b], ahead_in.at[c, k], ahead_send.at[b], ahead_recv.at[c, k], prv, user)

    def send_spill(k, it):
        for side in range(2):
            send(
                tc.at[it, k],
                spill_in.at[it, c, k],
                spill_send.at[side, it, k],
                spill_recv.at[it, c, k],
                nxt,
                side,
            )

    def wait_for(dst, sem):
        pltpu.make_async_copy(dst, dst, sem).wait()

    def gather_block(b, it):
        side, k = SPILLED[b]
        wait_for(spill_in.at[it, side, k], spill_recv.at[it, side, k])
        total = (tr[it, b] + other_in[it, b]) + spill_in[it, side, k]
        old = qq[b, it * PROBES : (it + 1) * PROBES]
        qq[b, (it + 1) * PROBES : (it + 2) * PROBES] = total * (alive[b] * (1.0 / UNIT)) - old

    def gather_ahead(k):
        for side in range(2):
            wait_for(ahead_in.at[side, k], ahead_recv.at[side, k])
        total = (ahead_in[0, k] + ahead_in[1, k]) + tc[0, k]
        qn[1, k] = total * (geo_r[4 * k + 3 : 4 * k + 4] * (1.0 / UNIT)) - qn[0, k]

    for quarter in range(4):
        across_part(ORDER[0], quarter, 0)
    for at, n in enumerate(ORDER):
        then = ORDER[at + 1] if at + 1 < len(ORDER) else None
        if at == 2:
            wait_for(qn.at[0], q_recv)
            for k in range(2):
                vnext[k] = two_parts(qn[0, k])
        for chunk in range(CHUNKS):
            if at == 1 and chunk == CHUNKS // 2:
                wait_for(geo_r, geo_recv)
                for k in range(2):
                    column_features(geo_r[4 * k : 4 * k + 4], 2 + k)
            build(n, chunk, at % 2)
            if at == 1:
                if chunk >= CHUNKS // 2 and chunk % 4 == 1:
                    across_part(then, (chunk - CHUNKS // 2) // 4, (at + 1) % 2)
            elif chunk % 8 == 3 and then is not None:
                across_part(then, chunk // 8, (at + 1) % 2)
            if chunk % 8 == 7 and at > 0:
                apply(ORDER[at - 1], chunk // 8, 0)
        if at == 4:
            send_spill(1, 0)
        if at == 7:
            send_spill(0, 0)
        if at == 8:
            send_rows(3, 4, 0)
            send_ahead(3)
        if at == 9:
            send_rows(2, 3, 0)
            send_ahead(2)
    for quarter in range(4):
        apply(ORDER[-1], quarter, 0)
    send_rows(0, 2, 0)
    send_ahead(1)
    send_ahead(0)

    def spread(turn, me, count, target):
        src, dst = tile.at[turn], sums.at[turn]

        def one(step, carry):
            pltpu.make_async_remote_copy(
                src_ref=src,
                dst_ref=dst.at[me],
                send_sem=red_send.at[turn],
                recv_sem=red_recv.at[turn],
                device_id=target(step),
                device_id_type=MESH,
            ).start()
            return carry

        lax.fori_loop(1, count, one, 0)
        dst[me] = src[...]

    def total_of(turn, count):
        everything = sums.at[turn, pl.ds(0, count - 1)]
        pltpu.make_async_copy(everything, everything, red_recv.at[turn]).wait()
        parts = [sums[turn, at] for at in range(count)]
        while len(parts) > 1:
            parts = [functools.reduce(jnp.add, parts[at : at + 2]) for at in range(0, len(parts), 2)]
        return parts[0]

    def rows_in(low, high, it):
        wait_for(other_in.at[it, low:high], other_recv.at[it, low])

    def ready(b):
        gather_block(b, 0)
        vrow[b] = two_parts(qq[b, PROBES : 2 * PROBES])

    def second(n):
        for quarter in range(4):
            apply(n, quarter, 1)

    rows_in(3, 4, 0)
    ready(3)
    rows_in(2, 3, 0)
    ready(2)
    second(0)
    rows_in(0, 2, 0)
    ready(1)
    ready(0)

    for n in range(1, 5):
        second(n)

    tile[...] = jnp.zeros_like(tile)
    gram = jnp.zeros((6 * PROBES, 6 * PROBES), f32)
    for b in range(2):
        pair = qq[2 * c + b, 0 : 2 * PROBES]
        parts = jnp.concatenate([piece.astype(bf16) for piece in split(pair, 3)], axis=0)
        gram += lax.dot_general(parts, parts, NT, preferred_element_type=f32)
    gram = gram[0:16] + gram[16:32] + gram[32:48]
    gram = gram[:, 0:16] + gram[:, 16:32] + gram[:, 32:48]
    tile[0, :, 0:16] = gram[0:PROBES]
    tile[0, :, 16:32] = gram[PROBES:]

    for k in range(2):
        gather_ahead(k)
        vnext[k] = two_parts(qn[1, k])
    for n in range(5, 10):
        second(n)

    part = jnp.zeros((2 * PROBES, 2 * PROBES), f32)
    for b in range(BLOCKS):
        part += lax.dot_general(vrow[b], two_parts(tr[1, b]), NT, preferred_element_type=f32)
    for k in range(2):
        part += lax.dot_general(vnext[k], two_parts(tc[1, k]), NT, preferred_element_type=f32)
    part = part[:PROBES] + part[PROBES:]
    part = part[:, :PROBES] + part[:, PROBES:]
    tile[0, :, 32:40] = part * (1.0 / UNIT)
    send(tile.at[0], sums.at[0, 0], red_send.at[0], red_recv.at[0], g, 1 - c)
    wait_for(sums.at[0, 0], red_recv.at[0])
    tile[1] = tile[0] + sums[0, 0]
    spread(1, inplane, plane, in_plane)
    for k in range(2):
        send_spill(k, 1)
    send_rows(0, 4, 1)
    tile[2] = total_of(1, plane)
    spread(2, z, zs, along_z)

    rows_in(0, 4, 1)
    for b in range(BLOCKS):
        gather_block(b, 1)
        for k in range(3 * PROBES):
            rhs[b, k] = jnp.broadcast_to(qq[b, k : k + 1], (PROBES, SLOTS))

    totals = total_of(2, zs)
    h00, h01, h11 = totals[:, 0:8], totals[:, 8:16], totals[:, 24:32]
    curv_inv = inverse(level * h00 + sill * h01)
    left = mm(curv_inv, totals[:, 0:40])
    alpha, m2, m1, m12 = (left[:, at : at + PROBES] for at in (0, 8, 24, 32))
    alpha_t = mm(h00, curv_inv)
    w_t = sill * mm(h01, curv_inv)
    middle = mm(h01, m2)
    n_fwd = sill * (mm(h00, m1) - middle)
    n_t = sill * (mm(h11, alpha) - middle)
    beta = sill * mm(curv_inv, n_t)
    beta_t = sill * mm(n_fwd, curv_inv)
    new = mm(h00, beta)
    inner = mm(h00, m12 - m1) - mm(h01, m1)
    curv = level * new - sill * mm(n_fwd, sill * m2 + beta) + sill**3 * mm(inner, alpha)
    x_y = mm(new, eliminate(curv, jnp.concatenate([w_t + beta_t, sill * alpha_t], axis=1)))
    x_t, y_t = x_y[:, :PROBES], x_y[:, PROBES:]
    top = (alpha_t + x_t, -y_t)
    low = (w_t - level * x_t, level * y_t - sill * x_t - sill * alpha_t, sill * y_t)
    for h, weights in enumerate((top, low)):
        columns = [part[:, k : k + 1] for part in weights for k in range(PROBES)]
        for b in range(BLOCKS):
            terms = [column * rhs[b, k] for k, column in enumerate(columns)]
            while len(terms) > 1:
                terms = [functools.reduce(jnp.add, terms[at : at + 2]) for at in range(0, len(terms), 2)]
            out_ref[h * PROBES : (h + 1) * PROBES, b * SLOTS : (b + 1) * SLOTS] = terms[0]

    for copy in sends:
        copy.wait_send()
    for turn, count in ((1, plane), (2, zs)):
        everything = sums.at[turn, pl.ds(0, count - 1)]
        pltpu.make_async_copy(everything, everything, red_send.at[turn]).wait()


def on_device(groups, plane, right_side, coords, counts, pair_list):
    del pair_list
    ring = groups // plane * 2
    block = (BLOCKS, PROBES, SLOTS)
    dma = pltpu.SemaphoreType.DMA
    width = right_side.shape[1]
    shape = jax.ShapeDtypeStruct((2 * PROBES, width), f32)
    anywhere = pl.BlockSpec(memory_space=pl.ANY)
    vmem = pl.BlockSpec(memory_space=pltpu.VMEM)
    both = pl.pallas_call(
        functools.partial(kernel, groups, plane),
        out_shape=shape,
        in_specs=[anywhere] * 3,
        out_specs=vmem,
        scratch_shapes=[
            pltpu.SMEM((BLOCKS,), jnp.int32),
            pltpu.VMEM((3, width), f32),
            pltpu.VMEM(block, f32),
            pltpu.VMEM((PROBES, SLOTS), f32),
            pltpu.VMEM((PROBES, SLOTS), f32),
            pltpu.VMEM((2, PROBES, SLOTS), f32),
            pltpu.VMEM((BLOCKS, 3 * PROBES, SLOTS), f32),
            pltpu.VMEM((2, 2, PROBES, SLOTS), f32),
            pltpu.VMEM((BLOCKS, 1, SLOTS), f32),
            pltpu.VMEM((BLOCKS, 128, SLOTS), f32),
            pltpu.VMEM((BLOCKS, SLOTS, 128), f32),
            pltpu.VMEM((BLOCKS, SLOTS, 128), bf16),
            pltpu.VMEM((BLOCKS, 128, SLOTS), f32),
            pltpu.VMEM((BLOCKS, 128, SLOTS), bf16),
            pltpu.VMEM((BLOCKS, 1, SLOTS), f32),
            pltpu.VMEM((BLOCKS, 2 * PROBES, SLOTS), bf16),
            pltpu.VMEM((2, 2 * PROBES, SLOTS), bf16),
            pltpu.VMEM((len(ORDER), SLOTS, 2 * SLOTS), bf16),
            pltpu.VMEM((2, SLOTS, SLOTS), f32),
            pltpu.VMEM((2,) + block, f32),
            pltpu.VMEM((2, 2, PROBES, SLOTS), f32),
            pltpu.VMEM((2,) + block, f32),
            pltpu.VMEM((2, 2, 2, PROBES, SLOTS), f32),
            pltpu.VMEM((2, 2, PROBES, SLOTS), f32),
            pltpu.VMEM((3, 8, 128), f32),
            pltpu.VMEM((3, max(plane, ring), 8, 128), f32),
            pltpu.VMEM((BLOCKS, 3 * PROBES, PROBES, SLOTS), f32),
            dma((6,)),
            dma,
            dma,
            dma,
            dma,
            dma((2, BLOCKS)),
            dma((BLOCKS,)),
            dma((2, 2, 2)),
            dma((2, BLOCKS)),
            dma((2, 2, 2)),
            dma((2, 2)),
            dma((3,)),
            dma((3,)),
        ],
        compiler_params=pltpu.CompilerParams(
            collective_id=0, has_side_effects=True, vmem_limit_bytes=60 << 20
        ),
        name="block_cg",
    )(right_side, coords, counts)
    return both[:PROBES], both[PROBES:]


def solution(mesh):
    groups = mesh.shape["blk"]
    plane = 16 if groups % 16 == 0 else 2
    placed = (P(None, "blk"), P(None, "blk"), P("blk"), P(None, ("blk", "rep")))
    return jax.shard_map(
        functools.partial(on_device, groups, plane),
        mesh=mesh,
        in_specs=placed,
        out_specs=(P(None, "blk"), P(None, "blk")),
        check_vma=False,
    )
```

```python
import functools
import math

import jax
import jax.numpy as jnp
from jax import lax
from jax.experimental import pallas as pl
from jax.experimental.pallas import tpu as pltpu
from jax.sharding import PartitionSpec as P

SPAN = 4
BLOCKS = 4
SLOTS = 512
PROBES = 8
FAR = 5

sill = 0.1 / SPAN
nugget = 0.5
level = nugget + sill

KAPPA = math.sqrt(3.0) / (0.5 * SPAN)
REACH = SPAN * KAPPA
MATERN_ROOT = 1.0
TAPER_ROOT = KAPPA * SPAN / 4.0
UNIT = REACH**4 * math.exp(REACH) * MATERN_ROOT * TAPER_ROOT

ROWS = ((3, -1), (3, 0), (2, 1), (1, 1), (0, 1))
COLS = ((3, -1), (0, 2), (0, 1), (0, 1), (0, 1))
KEPT = ((1, 0), (0, 1), (0, 0), (0, 0), (0, 0))
DIAGONAL = (0, 4)
SPILLED = ((0, 0), (1, 0), (1, 1), (0, 1))
ORDER = (0, 1, 5, 6, 7, 8, 9, 2, 3, 4)
CHUNK = 16
CHUNKS = SLOTS // CHUNK
XROW = 32

f32 = jnp.float32
bf16 = jnp.bfloat16
MESH = pl.DeviceIdType.MESH
NT = (((1,), (1,)), ((), ()))


def split(x, parts):
    out = []
    for _ in range(parts - 1):
        piece = x.astype(bf16).astype(f32)
        out.append(piece)
        x = x - piece
    out.append(x.astype(bf16).astype(f32))
    return out


def two_parts(x):
    high = x.astype(bf16)
    low = (x - high.astype(f32)).astype(bf16)
    return jnp.concatenate([high, low], axis=0)


def mm(a, b):
    terms = [a[:, k : k + 1] * b[k : k + 1] for k in range(PROBES)]
    while len(terms) > 1:
        terms = [functools.reduce(jnp.add, terms[at : at + 2]) for at in range(0, len(terms), 2)]
    return terms[0]


def inverse(matrix):
    rows = lax.broadcasted_iota(jnp.int32, (PROBES, PROBES), 0)
    eye = (rows == lax.broadcasted_iota(jnp.int32, (PROBES, PROBES), 1)).astype(f32)
    return eliminate(matrix, eye)


def eliminate(matrix, rhs):
    work = jnp.concatenate([matrix, rhs], axis=1)
    rows = lax.broadcasted_iota(jnp.int32, work.shape, 0)
    for k in range(PROBES):
        pivot = work[k : k + 1, k : k + 1]
        scaled = work[k : k + 1, :] / pivot
        column = jnp.broadcast_to(work[:, k : k + 1], work.shape)
        work = jnp.where(rows == k, scaled, work - column * scaled)
    return work[:, PROBES:]


def kernel(
    groups,
    plane,
    rs_ref,
    co_ref,
    cnt_ref,
    out_ref,
    cnt,
    co,
    geo_s,
    geo_out,
    geo_r,
    q_out,
    qq,
    qn,
    alive,
    lraw,
    xc,
    lfeat,
    rraw,
    rfeat,
    xr,
    vrow,
    vnext,
    kc,
    yzs,
    tr,
    tc,
    other_in,
    spill_in,
    ahead_in,
    tile,
    flat,
    sums,
    rhs,
    local_sem,
    geo_send,
    geo_recv,
    q_send,
    q_recv,
    mine_send,
    ahead_send,
    spill_send,
    other_recv,
    spill_recv,
    ahead_recv,
    red_send,
    red_recv,
):
    g = lax.axis_index("blk")
    c = lax.axis_index("rep")
    nxt = lax.rem(g + 1, groups)
    prv = lax.rem(g + groups - 1, groups)
    zs = groups // plane
    z, inplane = g // plane, lax.rem(g, plane)
    ring = zs * 2
    place = z * 2 + c

    def in_plane(k):
        return {"blk": z * plane + lax.rem(inplane + k, plane), "rep": c}

    def along_z(k):
        return {"blk": lax.rem(z + k, zs) * plane + inplane, "rep": c}

    def across(k):
        at = lax.rem(place + k, ring)
        return {"blk": (at // 2) * plane + inplane, "rep": lax.rem(at, 2)}

    def column(k):
        return c if k == 0 else 3 - c

    loads = [
        pltpu.make_async_copy(co_ref, co, local_sem.at[1]),
        pltpu.make_async_copy(cnt_ref, cnt, local_sem.at[0]),
    ]
    for b in range(BLOCKS):
        loads.append(
            pltpu.make_async_copy(
                rs_ref.at[:, pl.ds(b * SLOTS, SLOTS)], qq.at[b, 0:PROBES], local_sem.at[2 + b]
            )
        )
    for load in loads:
        load.start()

    barrier = pltpu.get_barrier_semaphore()

    def greet_plane(k, carry):
        pl.semaphore_signal(barrier, inc=1, device_id=in_plane(k), device_id_type=MESH)
        return carry

    def greet_across(k, carry):
        pl.semaphore_signal(barrier, inc=1, device_id=across(k), device_id_type=MESH)
        return carry

    for near in (prv, nxt):
        for side in (0, 1):
            pl.semaphore_signal(
                barrier, inc=1, device_id={"blk": near, "rep": side}, device_id_type=MESH
            )
    lax.fori_loop(1, ring, greet_across, 0)
    lax.fori_loop(1, plane, greet_plane, 0)

    for load in loads:
        load.wait()

    slot = lax.broadcasted_iota(jnp.int32, (1, SLOTS), 1)
    for b in range(BLOCKS):
        live = (slot < cnt[b]).astype(f32)
        alive[b] = live
        geo_s[b, 0:3] = co[:, b * SLOTS : (b + 1) * SLOTS]
        geo_s[b, 3:4] = live
        qq[b, 0:PROBES] = qq[b, 0:PROBES] * live

    pl.semaphore_wait(barrier, 4 + plane - 1 + ring - 1)

    def remote(src, dst, send_sem, recv_sem, blk, rep):
        return pltpu.make_async_remote_copy(
            src_ref=src,
            dst_ref=dst,
            send_sem=send_sem,
            recv_sem=recv_sem,
            device_id={"blk": blk, "rep": rep},
            device_id_type=MESH,
        )

    sends = []

    def send(*args):
        copy = remote(*args)
        copy.start()
        sends.append(copy)

    for k in range(2):
        geo_out[4 * k : 4 * k + 4] = geo_s[column(k), 0:4]
        q_out[k] = qq[column(k), 0:PROBES]
    send(geo_out, geo_r, geo_send, geo_recv, prv, c)
    send(q_out, qn.at[0], q_send, q_recv, prv, c)

    origin = geo_s[0, 0:1, 0:1]
    ones = jnp.ones((1, SLOTS), f32)

    def features(geo):
        x = (geo[0:1] - origin) * KAPPA
        y = (geo[1:2] - 0.5) * KAPPA
        w = (geo[2:3] - 0.5) * KAPPA
        return x, split(y, 3), split(w, 3), split(y * y + w * w, 3)

    def row_features(b):
        x, ys, ws, ns = features(geo_s[b])
        rows = []
        for q in (ys, ws):
            rows += [-2.0 * q[k] for k in (0, 0, 1, 1, 0, 2)]
        rows += ns + [ones] * 3
        for k, row in enumerate(rows):
            lraw[b, k : k + 1] = row
        lraw[b, XROW : XROW + 1] = x
        turned = lraw[b].T
        xc[b] = turned
        lfeat[b] = turned.astype(bf16)

    def column_features(geo, at):
        x, ys, ws, ns = features(geo)
        rows = []
        for q in (ys, ws):
            rows += [q[k] for k in (0, 1, 0, 1, 2, 0)]
        rows += [ones] * 3 + ns
        for k, row in enumerate(rows):
            rraw[at, k : k + 1] = row
        rfeat[at] = rraw[at].astype(bf16)
        xr[at] = x

    lraw[...] = jnp.zeros_like(lraw)
    rraw[...] = jnp.zeros_like(rraw)
    for k in range(2):
        column_features(geo_s[column(k)], k)
    for b in reversed(range(BLOCKS)):
        row_features(b)
        vrow[b] = two_parts(qq[b, 0:PROBES])

    def pick(table, n):
        low, step = table[n % 5]
        return low + step * c if step else low

    def kept(n):
        return pick(KEPT, n) + 2 * (n // 5)

    def build(n, chunk, half):
        s = pl.ds(chunk * CHUNK, CHUNK)
        along = xc[pick(ROWS, n), s, XROW : XROW + 1] - xr[kept(n)]
        square = jnp.maximum(along * along + yzs[half, s], 1e-12)
        dist = square * lax.rsqrt(square)
        inside = jnp.maximum(REACH - dist, 0.0)
        decay = jnp.exp(inside)
        twice = inside * inside
        value = (twice * twice) * decay * ((dist + MATERN_ROOT) * (dist + TAPER_ROOT))
        high = value.astype(bf16)
        kc[n, s, 0:SLOTS] = high
        kc[n, s, SLOTS:] = (value - high.astype(f32)).astype(bf16)

    def across_part(n, quarter, half):
        s = pl.ds(quarter * 128, 128)
        yzs[half, s] = jnp.dot(
            lfeat[pick(ROWS, n), s], rfeat[kept(n)], preferred_element_type=f32
        )

    def apply(n, quarter, it):
        i = pick(ROWS, n)
        h = quarter % 2
        s = pl.ds(h * 256, 256)
        if quarter < 2 and n in DIAGONAL:
            return
        if quarter < 2:
            both = jnp.dot(
                vrow[i, :, h * 256 : h * 256 + 256], kc[n, s], preferred_element_type=f32
            )
            both = both[:, :SLOTS] + both[:, SLOTS:]
            part = both[:PROBES] + both[PROBES:]
            if n < 5:
                tr[it, pick(COLS, n)] += part
            else:
                tc[it, pick(KEPT, n)] += part
        else:
            vec = vrow[pick(COLS, n)] if n < 5 else vnext[pick(KEPT, n)]
            both = lax.dot_general(vec, kc[n, s, 0:SLOTS], NT, preferred_element_type=f32)
            both += lax.dot_general(vec, kc[n, s, SLOTS:], NT, preferred_element_type=f32)
            tr[it, i, :, h * 256 : h * 256 + 256] += both[:PROBES] + both[PROBES:]

    tr[...] = jnp.zeros_like(tr)
    tc[...] = jnp.zeros_like(tc)

    def send_rows(low, high, it):
        send(
            tr.at[it, low:high],
            other_in.at[it, low:high],
            mine_send.at[it, low],
            other_recv.at[it, low],
            g,
            1 - c,
        )

    def send_ahead(b):
        k, user = {0: (0, 0), 3: (1, 0), 1: (0, 1), 2: (1, 1)}[b]
        send(tr.at[0, b], ahead_in.at[c, k], ahead_send.at[b], ahead_recv.at[c, k], prv, user)

    def send_spill(k, it):
        for side in range(2):
            send(
                tc.at[it, k],
                spill_in.at[it, c, k],
                spill_send.at[side, it, k],
                spill_recv.at[it, c, k],
                nxt,
                side,
            )

    def wait_for(dst, sem):
        pltpu.make_async_copy(dst, dst, sem).wait()

    def gather_block(b, it):
        side, k = SPILLED[b]
        wait_for(spill_in.at[it, side, k], spill_recv.at[it, side, k])
        total = (tr[it, b] + other_in[it, b]) + spill_in[it, side, k]
        old = qq[b, it * PROBES : (it + 1) * PROBES]
        qq[b, (it + 1) * PROBES : (it + 2) * PROBES] = total * (alive[b] * (1.0 / UNIT)) - old

    def gather_ahead(k):
        for side in range(2):
            wait_for(ahead_in.at[side, k], ahead_recv.at[side, k])
        total = (ahead_in[0, k] + ahead_in[1, k]) + tc[0, k]
        qn[1, k] = total * (geo_r[4 * k + 3 : 4 * k + 4] * (1.0 / UNIT)) - qn[0, k]

    for quarter in range(4):
        across_part(ORDER[0], quarter, 0)
    for at, n in enumerate(ORDER):
        then = ORDER[at + 1] if at + 1 < len(ORDER) else None
        if at == 2:
            wait_for(qn.at[0], q_recv)
            for k in range(2):
                vnext[k] = two_parts(qn[0, k])
        for chunk in range(CHUNKS):
            if at == 1 and chunk == CHUNKS - 8:
                wait_for(geo_r, geo_recv)
                for k in range(2):
                    column_features(geo_r[4 * k : 4 * k + 4], 2 + k)
            build(n, chunk, at % 2)
            if at == 1:
                if chunk >= CHUNKS - 8 and chunk % 2 == 1:
                    across_part(then, (chunk - CHUNKS + 8) // 2, (at + 1) % 2)
            elif chunk % 8 == 3 and then is not None:
                across_part(then, chunk // 8, (at + 1) % 2)
            if chunk % 8 == 7 and at > 0:
                apply(ORDER[at - 1], chunk // 8, 0)
        if at == 4:
            send_spill(1, 0)
        if at == 7:
            send_spill(0, 0)
        if at == 8:
            send_rows(3, 4, 0)
            send_ahead(3)
        if at == 9:
            send_rows(2, 3, 0)
            send_ahead(2)
    for quarter in range(4):
        apply(ORDER[-1], quarter, 0)
    send_rows(0, 2, 0)
    send_ahead(1)
    send_ahead(0)

    def spread(turn, me, count, target):
        src, dst = flat.at[turn], sums.at[turn]

        def one(step, carry):
            pltpu.make_async_remote_copy(
                src_ref=src,
                dst_ref=dst.at[me],
                send_sem=red_send.at[turn],
                recv_sem=red_recv.at[turn],
                device_id=target(step),
                device_id_type=MESH,
            ).start()
            return carry

        lax.fori_loop(1, count, one, 0)
        dst[me] = src[...]

    def total_of(turn, count):
        everything = sums.at[turn, pl.ds(0, count - 1)]
        pltpu.make_async_copy(everything, everything, red_recv.at[turn]).wait()
        parts = [sums[turn, at] for at in range(count)]
        while len(parts) > 1:
            parts = [functools.reduce(jnp.add, parts[at : at + 2]) for at in range(0, len(parts), 2)]
        return parts[0]

    def rows_in(low, high, it):
        wait_for(other_in.at[it, low:high], other_recv.at[it, low])

    def ready(b):
        gather_block(b, 0)
        vrow[b] = two_parts(qq[b, PROBES : 2 * PROBES])

    def second(n):
        for quarter in range(4):
            apply(n, quarter, 1)

    rows_in(3, 4, 0)
    ready(3)
    rows_in(2, 3, 0)
    ready(2)
    second(0)
    rows_in(0, 2, 0)
    ready(1)
    ready(0)

    for n in range(1, 5):
        second(n)

    tile[...] = jnp.zeros_like(tile)
    gram = jnp.zeros((6 * PROBES, 6 * PROBES), f32)
    for b in range(2):
        pair = qq[2 * c + b, 0 : 2 * PROBES]
        parts = jnp.concatenate([piece.astype(bf16) for piece in split(pair, 3)], axis=0)
        gram += lax.dot_general(parts, parts, NT, preferred_element_type=f32)
    gram = gram[0:16] + gram[16:32] + gram[32:48]
    gram = gram[:, 0:16] + gram[:, 16:32] + gram[:, 32:48]
    tile[0, :, 0:16] = gram[0:PROBES]
    tile[0, :, 16:24] = gram[PROBES:, PROBES:]

    for k in range(2):
        gather_ahead(k)
        vnext[k] = two_parts(qn[1, k])
    for n in range(5, 10):
        second(n)

    part = jnp.zeros((2 * PROBES, 2 * PROBES), f32)
    for b in range(BLOCKS):
        part += lax.dot_general(vrow[b], two_parts(tr[1, b]), NT, preferred_element_type=f32)
    for k in range(2):
        part += lax.dot_general(vnext[k], two_parts(tc[1, k]), NT, preferred_element_type=f32)
    part = part[:PROBES] + part[PROBES:]
    part = part[:, :PROBES] + part[:, PROBES:]
    tile[0, :, 24:32] = part * (1.0 / UNIT)
    for i in range(PROBES):
        wide = slice(32 * (i % 4), 32 * (i % 4) + 32)
        flat[0, i // 4 : i // 4 + 1, wide] = tile[0, i : i + 1, 0:32]
    send(flat.at[0], sums.at[0, 0], red_send.at[0], red_recv.at[0], g, 1 - c)
    wait_for(sums.at[0, 0], red_recv.at[0])
    flat[1] = flat[0] + sums[0, 0]
    spread(1, inplane, plane, in_plane)
    for k in range(2):
        send_spill(k, 1)
    send_rows(0, 4, 1)
    flat[2] = total_of(1, plane)
    spread(2, z, zs, along_z)

    rows_in(0, 4, 1)
    for b in range(BLOCKS):
        gather_block(b, 1)
        for k in range(3 * PROBES):
            rhs[b, k] = jnp.broadcast_to(qq[b, k : k + 1], (PROBES, SLOTS))

    flat[3] = total_of(2, zs)
    for i in range(PROBES):
        wide = slice(32 * (i % 4), 32 * (i % 4) + 32)
        tile[0, i : i + 1, 0:32] = flat[3, i // 4 : i // 4 + 1, wide]
    totals = tile[0, :, 0:32]
    h00, h01, h11 = totals[:, 0:8], totals[:, 8:16], totals[:, 16:24]
    curv_inv = inverse(level * h00 + sill * h01)
    left = mm(curv_inv, totals)
    alpha, m2, m1, m12 = (left[:, at : at + PROBES] for at in (0, 8, 16, 24))
    alpha_t = mm(h00, curv_inv)
    w_t = sill * mm(h01, curv_inv)
    middle = mm(h01, m2)
    n_fwd = sill * (mm(h00, m1) - middle)
    n_t = sill * (mm(h11, alpha) - middle)
    beta = sill * mm(curv_inv, n_t)
    beta_t = sill * mm(n_fwd, curv_inv)
    new = mm(h00, beta)
    inner = mm(h00, m12 - m1) - mm(h01, m1)
    curv = level * new - sill * mm(n_fwd, sill * m2 + beta) + sill**3 * mm(inner, alpha)
    x_y = mm(new, eliminate(curv, jnp.concatenate([w_t + beta_t, sill * alpha_t], axis=1)))
    x_t, y_t = x_y[:, :PROBES], x_y[:, PROBES:]
    top = (alpha_t + x_t, -y_t)
    low = (w_t - level * x_t, level * y_t - sill * x_t - sill * alpha_t, sill * y_t)
    for h, weights in enumerate((top, low)):
        columns = [part[:, k : k + 1] for part in weights for k in range(PROBES)]
        for b in range(BLOCKS):
            terms = [column * rhs[b, k] for k, column in enumerate(columns)]
            while len(terms) > 1:
                terms = [functools.reduce(jnp.add, terms[at : at + 2]) for at in range(0, len(terms), 2)]
            out_ref[h * PROBES : (h + 1) * PROBES, b * SLOTS : (b + 1) * SLOTS] = terms[0]

    for copy in sends:
        copy.wait_send()
    for turn, count in ((1, plane), (2, zs)):
        everything = sums.at[turn, pl.ds(0, count - 1)]
        pltpu.make_async_copy(everything, everything, red_send.at[turn]).wait()


def on_device(groups, plane, right_side, coords, counts, pair_list):
    del pair_list
    ring = groups // plane * 2
    block = (BLOCKS, PROBES, SLOTS)
    dma = pltpu.SemaphoreType.DMA
    width = right_side.shape[1]
    shape = jax.ShapeDtypeStruct((2 * PROBES, width), f32)
    anywhere = pl.BlockSpec(memory_space=pl.ANY)
    vmem = pl.BlockSpec(memory_space=pltpu.VMEM)
    both = pl.pallas_call(
        functools.partial(kernel, groups, plane),
        out_shape=shape,
        in_specs=[anywhere] * 3,
        out_specs=vmem,
        scratch_shapes=[
            pltpu.SMEM((BLOCKS,), jnp.int32),
            pltpu.VMEM((3, width), f32),
            pltpu.VMEM(block, f32),
            pltpu.VMEM((PROBES, SLOTS), f32),
            pltpu.VMEM((PROBES, SLOTS), f32),
            pltpu.VMEM((2, PROBES, SLOTS), f32),
            pltpu.VMEM((BLOCKS, 3 * PROBES, SLOTS), f32),
            pltpu.VMEM((2, 2, PROBES, SLOTS), f32),
            pltpu.VMEM((BLOCKS, 1, SLOTS), f32),
            pltpu.VMEM((BLOCKS, 128, SLOTS), f32),
            pltpu.VMEM((BLOCKS, SLOTS, 128), f32),
            pltpu.VMEM((BLOCKS, SLOTS, 128), bf16),
            pltpu.VMEM((BLOCKS, 128, SLOTS), f32),
            pltpu.VMEM((BLOCKS, 128, SLOTS), bf16),
            pltpu.VMEM((BLOCKS, 1, SLOTS), f32),
            pltpu.VMEM((BLOCKS, 2 * PROBES, SLOTS), bf16),
            pltpu.VMEM((2, 2 * PROBES, SLOTS), bf16),
            pltpu.VMEM((len(ORDER), SLOTS, 2 * SLOTS), bf16),
            pltpu.VMEM((2, SLOTS, SLOTS), f32),
            pltpu.VMEM((2,) + block, f32),
            pltpu.VMEM((2, 2, PROBES, SLOTS), f32),
            pltpu.VMEM((2,) + block, f32),
            pltpu.VMEM((2, 2, 2, PROBES, SLOTS), f32),
            pltpu.VMEM((2, 2, PROBES, SLOTS), f32),
            pltpu.VMEM((1, 8, 128), f32),
            pltpu.VMEM((4, 2, 128), f32),
            pltpu.VMEM((3, max(plane, ring), 2, 128), f32),
            pltpu.VMEM((BLOCKS, 3 * PROBES, PROBES, SLOTS), f32),
            dma((6,)),
            dma,
            dma,
            dma,
            dma,
            dma((2, BLOCKS)),
            dma((BLOCKS,)),
            dma((2, 2, 2)),
            dma((2, BLOCKS)),
            dma((2, 2, 2)),
            dma((2, 2)),
            dma((3,)),
            dma((3,)),
        ],
        compiler_params=pltpu.CompilerParams(
            collective_id=0, has_side_effects=True, vmem_limit_bytes=60 << 20
        ),
        name="block_cg",
    )(right_side, coords, counts)
    return both[:PROBES], both[PROBES:]


def solution(mesh):
    groups = mesh.shape["blk"]
    plane = 16 if groups % 16 == 0 else 2
    placed = (P(None, "blk"), P(None, "blk"), P("blk"), P(None, ("blk", "rep")))
    return jax.shard_map(
        functools.partial(on_device, groups, plane),
        mesh=mesh,
        in_specs=placed,
        out_specs=(P(None, "blk"), P(None, "blk")),
        check_vma=False,
    )
```
